128 devices in a mesh: row: 8 (over y_lo, z), col: 16 (over x, y_hi, core).
Axes of the slice: x: 4, y: 4 (y_hi: 2, y_lo: 2; y = y_hi * 2 + y_lo), z: 4, core: 2. Of those that a mesh axis runs over, the one named last changes fastest.
Arguments:
- hessian: float32 [16384, 8, 16, 128], P('row', None, 'col'), may hold values from -1 to 16, as said below
- weights: bfloat16 [512, 16384], P('col', 'row'), may hold values from -6 to 6
- codes: int32 [512, 8192], P('col', 'row'), may hold values from 0 to 255
- tile_map: int32 [32, 64], P('col', 'row'), may hold values from 0 to 511
- codebooks: float32 [512, 2, 256], replicated, may hold values from -6 to 6
Outputs:
- adjusted_codebooks: float32 [512, 2, 256], replicated
The draws below stay inside these ranges and needn't reach their ends.
Inputs may be any that keep to these rules, and one draw needn't show every extreme that they name: `hessian`: H is symmetric with a dominant positive diagonal.
All inputs are finite; a program needn't handle non-finite values.
Results may differ from the reference program's by a relative error of at most 0.0003.
Values sent between devices are 32-bit elements; how exact they have to be, the bound alone decides.
No kernel may reach another device: no remote copies, remote signals or barrier semaphores. Data moves between devices by JAX's collectives and lax.ppermute only.
A program may use at most 64 MiB of HBM per device.

```python
import math
import jax
import jax.numpy as jnp
from jax import lax

D = 16384
R = 512
CODES = 256
NB = 512
TILE_ROWS = 16
TILE_COLS = 256
STEPS = 2
N_ROW = 8
N_COL = 16


def draw_hessian(key, part):
    base_key = jax.random.fold_in(key, 23)
    scale_key, noise_key, diag_key = jax.random.split(base_key, 3)
    scales = jnp.exp(jax.random.uniform(scale_key, (D,), jnp.float32, math.log(0.5), math.log(2.0)))
    noise = jnp.clip(jax.random.normal(noise_key, (D, D), jnp.float32), -5.0, 5.0)
    damping = jax.random.uniform(diag_key, (D,), jnp.float32, 1.0, 1.5)
    symmetric = (noise + noise.T) * (0.3 / math.sqrt(2.0 * D))
    eye = (lax.broadcasted_iota(jnp.int32, (D, D), 0) == lax.broadcasted_iota(jnp.int32, (D, D), 1)).astype(jnp.float32)
    inner = symmetric + eye * damping[:, None]
    outer = scales[:, None] * scales[None, :]
    values = outer * inner
    return values.reshape(D, N_ROW, N_COL, D // (N_ROW * N_COL))


def touch_ends(result, stream_key, low, top_value):
    longest = result.shape.index(max(result.shape))
    spots = []
    for shift in (0, 1):
        where = [jax.random.randint(jax.random.fold_in(stream_key, axis), (), 0, length) for axis, length in enumerate(result.shape)]
        where[longest] = (where[longest] + shift) % result.shape[longest]
        spots.append(tuple(where))
    return result.at[spots[0]].set(low).at[spots[1]].set(top_value)


def block_levels(rng, dims, cuts, least, largest):
    def one(dim, blocks):
        steps = jax.random.uniform(jax.random.fold_in(jax.random.fold_in(rng, 6), dim), (blocks,), jnp.float32, least / len(cuts), largest / len(cuts))
        return jnp.repeat(jnp.exp(steps), dims[dim] // blocks).reshape((-1,) + (1,) * (len(dims) - dim - 1))

    gain = one(*cuts[0])
    for cut in cuts[1:]:
        gain = gain * one(*cut)
    return gain


def bell_draw(rng, dims, scale, most, shards=(), held_as=jnp.bfloat16):
    drawn = jax.random.normal(rng, dims, jnp.float32) * scale
    if len(shards) > 0:
        drawn = block_levels(rng, dims, shards, -0.22, 0.18) * drawn
    return jnp.clip(drawn, min=-most, max=most).astype(held_as)


def setup_inputs(seed: int = 0) -> dict:
    streams_of = jax.random.split(jax.random.key(seed), 6)
    hessian = draw_hessian(jax.random.fold_in(streams_of[5], 71), 0)
    weights = bell_draw(streams_of[1], (R, D), 1.0, 6.0, ((0, 16), (1, 8)))
    codes = touch_ends(jax.random.randint(streams_of[2], (R, D // 2), 0, CODES), jax.random.fold_in(streams_of[2], 1), 0, CODES - 1).astype(jnp.int32)
    tile_map = touch_ends(jax.random.randint(streams_of[3], (R // TILE_ROWS, D // TILE_COLS), 0, NB), jax.random.fold_in(streams_of[3], 1), 0, NB - 1).astype(jnp.int32)
    codebooks = bell_draw(streams_of[4], (NB, 2, CODES), 1.0, 6.0, (), jnp.float32)
    return {"hessian": hessian, "weights": weights, "codes": codes, "tile_map": tile_map, "codebooks": codebooks}


learn_rate = 0.01


def book_index(tile_map):
    spread = jnp.repeat(tile_map, TILE_ROWS, axis=0)
    return jnp.repeat(spread, TILE_COLS // 2, axis=1)


def reference(hessian, weights, codes, tile_map, codebooks):
    full_hessian = hessian.reshape(D, D)
    flat_index = (book_index(tile_map) * CODES + codes).astype(jnp.int32)
    for iteration in range(STEPS):
        table_even = codebooks[:, 0, :].reshape(-1)
        table_odd = codebooks[:, 1, :].reshape(-1)
        rebuilt = jnp.stack([table_even[flat_index], table_odd[flat_index]], axis=-1).reshape(R, D)
        error = rebuilt - weights.astype(jnp.float32)
        weight_grad = 2.0 * jnp.dot(error, full_hessian, precision=lax.Precision.HIGHEST)
        grad_even = jax.ops.segment_sum(weight_grad[:, 0::2].reshape(-1), flat_index.reshape(-1), NB * CODES)
        grad_odd = jax.ops.segment_sum(weight_grad[:, 1::2].reshape(-1), flat_index.reshape(-1), NB * CODES)
        book_grad = jnp.stack([grad_even.reshape(NB, CODES), grad_odd.reshape(NB, CODES)], axis=1)
        codebooks = codebooks - learn_rate * book_grad
    return codebooks
```

```python
import jax
import jax.numpy as jnp
from jax import lax
from jax.experimental import pallas as pl
from jax.experimental.pallas import tpu as pltpu
from jax.sharding import PartitionSpec as P

F32 = jnp.float32
BF16 = jnp.bfloat16
I32 = jnp.int32
LEARN_RATE = 0.01
BOTH = ("row", "col")
VMEM_LIMIT = 56 * 1024 * 1024


def partners(dx, dyh, dcore, dyl, dz):
    flip_col = dx * 4 + dyh * 2 + dcore
    flip_row = dyl * 4 + dz
    return [(i, i ^ (flip_row * 16 + flip_col)) for i in range(128)]


def swap(v, dx=0, dyh=0, dcore=0, dyl=0, dz=0):
    return lax.ppermute(v, BOTH, partners(dx, dyh, dcore, dyl, dz))


def lanes(x, index):
    return jnp.take_along_axis(x, index, axis=1, mode="promise_in_bounds")


def iota(shape, dim):
    return lax.broadcasted_iota(I32, shape, dim)


def split(x):
    high = x.astype(BF16)
    low = (x - high.astype(F32)).astype(BF16)
    return high, low


def dot_nt(a, b):
    return lax.dot_general(a, b, (((1,), (1,)), ((), ())), preferred_element_type=F32)


def dot_nn(a, b):
    return lax.dot_general(a, b, (((1,), (0,)), ((), ())), preferred_element_type=F32)


def pick(index, even0, even1, odd0, odd1, odd):
    low = index & 127
    upper = index >= 128
    even_value = jnp.where(upper, lanes(even1, low), lanes(even0, low))
    odd_value = jnp.where(upper, lanes(odd1, low), lanes(odd0, low))
    return jnp.where(odd, odd_value, even_value)


def first_kernel(tile_ref, weights_ref, codes_ref, books_ref, error_ref, piece_ref, own_ref):
    lane = iota((16, 128), 1)
    odd = (lane & 1) == 1
    for q in range(8):
        codes = [codes_ref[t * 16 : t * 16 + 16, q * 128 : q * 128 + 128] for t in range(2)]
        books = [books_ref[tile_ref[t, q]] for t in range(2)]
        for h in range(2):
            piece = 2 * q + h
            for t in range(2):
                tables = [
                    jnp.broadcast_to(books[t][c : c + 1, k * 128 : k * 128 + 128], (16, 128))
                    for c in range(2)
                    for k in range(2)
                ]
                index = lanes(codes[t], h * 64 + (lane >> 1))
                value = pick(index, *tables, odd)
                weight = weights_ref[t * 16 : t * 16 + 16, piece * 128 : piece * 128 + 128]
                error_ref[piece, t * 16 : t * 16 + 16, :] = value - weight.astype(F32)
            place = h * 64 + (lane & 63)
            piece_ref[piece, 0:16, :] = jnp.where(lane < 64, lanes(codes[0], place), lanes(codes[1], place))
            piece_ref[piece, 16:24, :] = jnp.where(iota((8, 128), 1) == 0, tile_ref[0, q], tile_ref[1, q])
    own_ref[0:32, :] = codes_ref[...]
    wide = iota((8, 1024), 1)
    for t in range(2):
        row = jnp.zeros((8, 1024), I32)
        for q in range(8):
            row = jnp.where(wide == q, tile_ref[t, q], row)
        if t == 0:
            kept = row
    own_ref[32:40, :] = jnp.where(iota((8, 1024), 0) == 0, kept, row)


def first(weights, codes, tile_map, codebooks):
    vmem = pl.BlockSpec(memory_space=pltpu.VMEM)
    return pl.pallas_call(
        first_kernel,
        out_shape=[
            jax.ShapeDtypeStruct((16, 32, 128), F32),
            jax.ShapeDtypeStruct((16, 24, 128), I32),
            jax.ShapeDtypeStruct((40, 1024), I32),
        ],
        in_specs=[pl.BlockSpec(memory_space=pltpu.SMEM), vmem, vmem, vmem],
        out_specs=[vmem, vmem, vmem],
    )(tile_map, weights, codes, codebooks)


def sort_kernel(col_ref, near_ref, far_ref, packed_ref, rows_ref, keys_ref):
    col = col_ref[0]
    for core, part_ref in ((0, near_ref), (1, far_ref)):
        for m in range(8):
            where_to = (2 * m + core) ^ col
            rows_ref[pl.ds(pl.multiple_of(where_to * 40, 8), 40), :] = part_ref[m]
    for r in range(16):
        for t in range(2):
            keys_ref[(r * 2 + t) * 16 : (r * 2 + t) * 16 + 16, :] = rows_ref[pl.ds(t * 16 + r, 16, stride=40), :]
    size = 64
    lane = iota((size, 128), 1)

    def chunk(n, carry):
        start = pl.multiple_of(n * size, size)
        key = (keys_ref[pl.ds(start, size), :] * 128 + lane).astype(F32)
        k = 2
        while k <= 128:
            j = k // 2
            while j >= 1:
                other = lanes(key, lane ^ j)
                rising = ((lane & k) == 0) == ((lane & j) == 0)
                key = jnp.where(rising, jnp.minimum(key, other), jnp.maximum(key, other))
                j //= 2
            k *= 2
        whole = key.astype(I32)
        packed = whole & 127
        for half in range(2):
            limit = (half * 128 + lane + 1) * 128
            count = jnp.zeros((size, 128), I32)
            for step in (64, 32, 16, 8, 4, 2, 1, 1):
                below = lanes(whole, count + (step - 1)) < limit
                count = jnp.where(below, count + step, count)
            packed = packed | (count << (8 + 8 * half))
        packed_ref[pl.ds(start, size), :] = packed
        return carry

    lax.fori_loop(0, 512 // size, chunk, 0)


def sort_codes(col, near, far):
    block = pl.BlockSpec((8, 40, 128), lambda q: (0, 0, q))
    return pl.pallas_call(
        sort_kernel,
        out_shape=jax.ShapeDtypeStruct((512, 1024), I32),
        grid=(8,),
        in_specs=[pl.BlockSpec(memory_space=pltpu.SMEM), block, block],
        out_specs=pl.BlockSpec((512, 128), lambda q: (0, q)),
        scratch_shapes=[pltpu.VMEM((640, 128), I32), pltpu.VMEM((512, 128), I32)],
    )(col, near, far)


def step_body(second, place_ref, hessian_ref, packed_ref, book_row_ref, refs):
    if second:
        (error_ref, piece_ref, near_ref, far_ref, book_col_ref), outs = refs[:5], refs[5:]
    else:
        (error_ref,), outs = refs[:1], refs[1:]
    keep_ref, send_ref, eh_ref, el_ref, hh_ref, hl_ref, sums_ref, table_ref = outs
    q = pl.program_id(0)
    place = place_ref[0]
    lane16 = iota((16, 128), 1)
    odd = (lane16 & 1) == 1

    @pl.when(q == 0)
    def _():
        if second:
            chosen = jnp.where((book_col_ref[...] ^ place) == iota((256, 512), 1), 1.0, 0.0).astype(BF16)
            total = jnp.zeros((256, 512), F32)
            for part, ref in ((0, near_ref), (1, far_ref)):
                high, low = split(ref[...])
                here = chosen[:, part * 256 : part * 256 + 256]
                total = total + dot_nn(here, high) + dot_nn(here, low)
            table_ref[...] = total

        def column(j, carry):
            if second:
                base = pl.multiple_of(j * 32, 32)
                tables = [
                    [table_ref[pl.ds(base + t * 16, 16), k * 128 : k * 128 + 128] for k in range(4)] for t in range(2)
                ]
            for r in range(16):
                if second:
                    codes = piece_ref[pl.ds(j * 384 + r, 16, stride=24), :]
                for t in range(2):
                    value = error_ref[pl.ds(j * 512 + t * 16 + r, 16, stride=32), :]
                    if second:
                        index = lanes(codes, t * 64 + (lane16 >> 1))
                        value = value - LEARN_RATE * pick(index, *tables[t], odd)
                    high, low = split(value)
                    rows = slice((r * 2 + t) * 16, (r * 2 + t) * 16 + 16)
                    eh_ref[j, rows, :] = high
                    el_ref[j, rows, :] = low
            return carry

        lax.fori_loop(0, 8, column, 0)

    for j in range(8):
        for parity in range(2):
            high, low = split(hessian_ref[pl.ds(parity * 8 + j, 128, stride=16), :])
            hh_ref[parity * 128 : parity * 128 + 128, j * 128 : j * 128 + 128] = high
            hl_ref[parity * 128 : parity * 128 + 128, j * 128 : j * 128 + 128] = low
    grad = jnp.zeros((512, 256), F32)
    for j in range(8):
        cut = slice(j * 128, j * 128 + 128)
        grad = grad + dot_nt(eh_ref[j], hh_ref[:, cut]) + dot_nt(el_ref[j], hh_ref[:, cut]) + dot_nt(eh_ref[j], hl_ref[:, cut])
    packed = packed_ref[...]
    source = packed & 127
    counts = [(packed >> 8) & 255, packed >> 16]
    running = jnp.where((iota((256, 128), 0) & 127) <= iota((256, 128), 1), 1.0, 0.0).astype(BF16)
    lane32 = iota((32, 128), 1)
    for c in range(2):
        ordered = lanes(grad[:, c * 128 : c * 128 + 128], source)
        prefix = dot_nn(jnp.concatenate(split(ordered), axis=1), running)
        upto = []
        for count in counts:
            value = jnp.where(count > 0, lanes(prefix, jnp.maximum(count - 1, 0)), 0.0)
            upto.append(value.reshape(16, 32, 128).sum(axis=0))
        before = [pltpu.roll(v, 1, 1) for v in upto]
        sums_ref[q, :, c * 256 : c * 256 + 128] = 2.0 * (upto[0] - jnp.where(lane32 == 0, 0.0, before[0]))
        sums_ref[q, :, c * 256 + 128 : c * 256 + 256] = 2.0 * (upto[1] - jnp.where(lane32 == 0, before[0], before[1]))

    @pl.when(q == 7)
    def _():
        chosen = jnp.where((iota((512, 256), 0) ^ place) == book_row_ref[...], 1.0, 0.0).astype(BF16)
        high, low = split(sums_ref[...].reshape(256, 512))
        total = dot_nn(chosen, high) + dot_nn(chosen, low)
        keep_ref[...] = total[0:256]
        send_ref[...] = total[256:512]


def step(second, place, hessian, packed, book_row, *rest):
    def kernel(place_ref, hessian_ref, packed_ref, book_row_ref, *refs):
        step_body(second, place_ref, hessian_ref, packed_ref, book_row_ref, refs)

    def whole(x):
        return pl.BlockSpec(x.shape, lambda q: (0,) * x.ndim)

    half = jax.ShapeDtypeStruct((256, 512), F32)
    return pl.pallas_call(
        kernel,
        out_shape=[half, half],
        grid=(8,),
        in_specs=[
            pl.BlockSpec(memory_space=pltpu.SMEM),
            pl.BlockSpec((2048, 128), lambda q: (q, 0)),
            pl.BlockSpec((512, 128), lambda q: (0, q)),
            whole(book_row),
        ]
        + [whole(x) for x in rest],
        out_specs=[pl.BlockSpec((256, 512), lambda q: (0, 0))] * 2,
        scratch_shapes=[
            pltpu.VMEM((8, 512, 128), BF16),
            pltpu.VMEM((8, 512, 128), BF16),
            pltpu.VMEM((256, 1024), BF16),
            pltpu.VMEM((256, 1024), BF16),
            pltpu.VMEM((8, 32, 512), F32),
            pltpu.VMEM((256, 512), F32),
        ],
        compiler_params=pltpu.CompilerParams(vmem_limit_bytes=VMEM_LIMIT),
    )(place, hessian, packed, book_row, *rest)


def last_kernel(place_ref, books_ref, near0_ref, far0_ref, near1_ref, far1_ref, out_ref):
    place = place_ref[0]
    for part, (a_ref, b_ref) in enumerate(((near0_ref, near1_ref), (far0_ref, far1_ref))):
        for k in range(4):
            start = pl.multiple_of((part * 256 + k * 64) ^ place, 64)
            for c in range(2):
                cut = (slice(k * 64, k * 64 + 64), slice(c * 256, c * 256 + 256))
                moved = LEARN_RATE * (a_ref[cut] + b_ref[cut])
                out_ref[pl.ds(start, 64), c, :] = books_ref[pl.ds(start, 64), c, :] - moved


def last(place, codebooks, *parts):
    vmem = pl.BlockSpec(memory_space=pltpu.VMEM)
    return pl.pallas_call(
        last_kernel,
        out_shape=jax.ShapeDtypeStruct((512, 2, 256), F32),
        in_specs=[pl.BlockSpec(memory_space=pltpu.SMEM)] + [vmem] * 5,
        out_specs=vmem,
    )(place, codebooks, *parts)


def sum_all(keep, send):
    half = keep + swap(send, dcore=1)
    quarter = [half[k * 64 : k * 64 + 64] for k in range(4)]
    got = [None] + [swap(quarter[k], dx=k) for k in (1, 2, 3)]
    s = (quarter[0] + got[2]) + (got[1] + got[3])
    got = [None] + [swap(s, dyl=k & 1, dyh=k >> 1) for k in (1, 2, 3)]
    s = (s + got[2]) + (got[1] + got[3])
    got = [None] + [swap(s, dz=k) for k in (1, 2, 3)]
    s = (s + got[2]) + (got[1] + got[3])
    near = jnp.concatenate([s] + [swap(s, dx=k) for k in (1, 2, 3)])
    return near, swap(near, dcore=1)


def per_device(hessian, weights, codes, tile_map, codebooks):
    col = lax.axis_index("col").astype(I32)
    place = ((col & 1) * 256 + (col >> 2) * 64).reshape(1)
    rows = hessian.reshape(16384, 128)
    error, piece, own = first(weights, codes, tile_map, codebooks)

    pair = jnp.stack([own, swap(own, dyh=1)])
    near = jnp.concatenate([pair] + [swap(pair, dx=k) for k in (1, 2, 3)])
    far = swap(near, dcore=1)
    packed = sort_codes(col.reshape(1), near, far)
    tiles = jnp.stack([near[:, 32:34, 0:8], far[:, 32:34, 0:8]], axis=1).reshape(16, 2, 8)
    same = (iota((16, 16), 0) ^ col) == iota((16, 16), 1)
    tiles = jnp.where(same[:, :, None, None], tiles[None], 0).sum(axis=1)
    book_row = tiles.transpose(2, 1, 0).reshape(1, 256)

    def spread(x):
        wide = jnp.broadcast_to(x[None], (8,) + x.shape).reshape((128,) + x.shape[1:])
        return lax.all_to_all(wide, BOTH, 0, 0, tiled=True)

    errors = spread(error).reshape(4096, 128)
    pieces = spread(piece)
    book_col = pieces.reshape(8, 16, 24, 128)[:, :, 16, 0:2].transpose(0, 2, 1).reshape(256, 1)
    pieces = pieces.reshape(3072, 128)

    near0, far0 = sum_all(*step(False, place, rows, packed, book_row, errors))
    near1, far1 = sum_all(*step(True, place, rows, packed, book_row, errors, pieces, near0, far0, book_col))
    return last(place, codebooks, near0, far0, near1, far1)


def solution(mesh):
    placed = (P("row", None, "col", None), P("col", "row"), P("col", "row"), P("col", "row"), P())
    return jax.shard_map(per_device, mesh=mesh, in_specs=placed, out_specs=P(), check_vma=False)
```

```python
import jax
import jax.numpy as jnp
from jax import lax
from jax.experimental import pallas as pl
from jax.experimental.pallas import tpu as pltpu
from jax.sharding import PartitionSpec as P

F32 = jnp.float32
BF16 = jnp.bfloat16
I32 = jnp.int32
LEARN_RATE = 0.01
BOTH = ("row", "col")
VMEM_LIMIT = 56 * 1024 * 1024


def partners(dx, dyh, dcore, dyl, dz):
    flip_col = dx * 4 + dyh * 2 + dcore
    flip_row = dyl * 4 + dz
    return [(i, i ^ (flip_row * 16 + flip_col)) for i in range(128)]


def swap(v, dx=0, dyh=0, dcore=0, dyl=0, dz=0):
    return lax.ppermute(v, BOTH, partners(dx, dyh, dcore, dyl, dz))


def lanes(x, index):
    return jnp.take_along_axis(x, index, axis=1, mode="promise_in_bounds")


def iota(shape, dim):
    return lax.broadcasted_iota(I32, shape, dim)


def split(x):
    high = x.astype(BF16)
    low = (x - high.astype(F32)).astype(BF16)
    return high, low


def dot_nt(a, b):
    return lax.dot_general(a, b, (((1,), (1,)), ((), ())), preferred_element_type=F32)


def dot_nn(a, b):
    return lax.dot_general(a, b, (((1,), (0,)), ((), ())), preferred_element_type=F32)


def whole(x):
    return pl.BlockSpec(x.shape, lambda *_: (0,) * x.ndim)


def in_vmem(n):
    return [pl.BlockSpec(memory_space=pltpu.VMEM)] * n


def in_smem():
    return pl.BlockSpec(memory_space=pltpu.SMEM)


def lookup(code, low_table, high_table):
    low = code & 127
    return jnp.where(code >= 128, lanes(high_table, low), lanes(low_table, low))


def part_pairs():
    lane = iota((256, 256), 1)
    return jnp.where(iota((256, 256), 0) == 2 * (lane & 127) + (lane >> 7), 1.0, 0.0).astype(BF16)


def tile_rows(start, tile, parity):
    return pl.ds(start + tile * 16 + parity, 8, stride=2)


def pieces_kernel(tile_ref, codes_ref, piece_ref, own_ref, held_ref):
    lane = iota((8, 128), 1)
    left = lane < 64
    for q in range(8):
        cut = slice(q * 128, q * 128 + 128)
        held_ref[q * 32 : q * 32 + 32, :] = codes_ref[:, cut]
        for t in range(2):
            even = held_ref[tile_rows(q * 32, t, 0), :]
            odd = held_ref[tile_rows(q * 32, t, 1), :]
            own_ref[t * 8 : t * 8 + 8, cut] = even
            own_ref[16 + t * 8 : 24 + t * 8, cut] = odd
            pair = [
                jnp.where(left, even, pltpu.roll(odd, 64, 1)),
                jnp.where(left, pltpu.roll(even, 64, 1), odd),
            ]
            for h in range(2):
                for copy in range(8):
                    piece_ref[copy, 2 * q + h, t * 8 : t * 8 + 8, :] = pair[h]
        books = jnp.where(lane == 0, tile_ref[0, q], tile_ref[1, q])
        for h in range(2):
            for copy in range(8):
                piece_ref[copy, 2 * q + h, 16:24, :] = books
    wide = iota((8, 1024), 1)
    rows = []
    for t in range(2):
        row = jnp.zeros((8, 1024), I32)
        for q in range(8):
            row = jnp.where(wide == q, tile_ref[t, q], row)
        rows.append(row)
    own_ref[32:40, :] = jnp.where(iota((8, 1024), 0) == 0, rows[0], rows[1])


def make_pieces(codes, tile_map):
    return pl.pallas_call(
        pieces_kernel,
        out_shape=[jax.ShapeDtypeStruct((8, 16, 24, 128), I32), jax.ShapeDtypeStruct((40, 1024), I32)],
        in_specs=[in_smem()] + in_vmem(1),
        out_specs=in_vmem(2),
        scratch_shapes=[pltpu.VMEM((256, 128), I32)],
    )(tile_map, codes)


def first_kernel(tile_ref, weights_ref, own_ref, books_ref, error_ref, weight_ref):
    parting = part_pairs()
    for q in range(8):
        parted = dot_nn(weights_ref[:, q * 256 : q * 256 + 256], parting)
        weight_ref[q * 64 : q * 64 + 32, :] = parted[:, 0:128]
        weight_ref[q * 64 + 32 : q * 64 + 64, :] = parted[:, 128:256]
    for q in range(8):
        for t in range(2):
            book = books_ref[tile_ref[t, q]]
            for c in range(2):
                tables = [jnp.broadcast_to(book[c : c + 1, k * 128 : k * 128 + 128], (8, 128)) for k in range(2)]
                for parity in range(2):
                    row = parity * 16 + t * 8
                    code = own_ref[row : row + 8, q * 128 : q * 128 + 128]
                    weight = weight_ref[tile_rows((q * 2 + c) * 32, t, parity), :]
                    error_ref[q * 2 + c, row : row + 8, :] = lookup(code, *tables) - weight


def first(weights, own, tile_map, codebooks):
    return pl.pallas_call(
        first_kernel,
        out_shape=jax.ShapeDtypeStruct((16, 32, 128), F32),
        in_specs=[in_smem()] + in_vmem(3),
        out_specs=in_vmem(1)[0],
        scratch_shapes=[pltpu.VMEM((512, 128), F32)],
    )(tile_map, weights, own, codebooks)


def sort_kernel(piece_ref, packed_ref):
    lane = iota((256, 128), 1)
    key = (piece_ref[:, 0:16, :].reshape(256, 128) * 128 + lane).astype(F32)
    k = 2
    while k <= 128:
        j = k // 2
        while j >= 1:
            lower = (lane & j) == 0
            other = jnp.where(lower, pltpu.roll(key, 128 - j, 1), pltpu.roll(key, j, 1))
            rising = ((lane & k) == 0) == lower
            key = jnp.where(rising, jnp.minimum(key, other), jnp.maximum(key, other))
            j //= 2
        k *= 2
    code = key.astype(I32)
    counts = []
    for half in range(2):
        limit = (half * 128 + lane + 1) * 128
        count = jnp.zeros((256, 128), I32)
        for step in (64, 32, 16, 8, 4, 2, 1, 1):
            below = lanes(code, count + (step - 1)) < limit
            count = jnp.where(below, count + step, count)
        counts.append(count)
    packed_ref[0] = (code & 127) | (counts[0] << 8) | (counts[1] << 16)


def sort_codes(pieces):
    return pl.pallas_call(
        sort_kernel,
        out_shape=jax.ShapeDtypeStruct((8, 256, 128), I32),
        grid=(8,),
        in_specs=[pl.BlockSpec((16, 24, 128), lambda j: (j, 0, 0))],
        out_specs=pl.BlockSpec((1, 256, 128), lambda j: (j, 0, 0)),
        compiler_params=pltpu.CompilerParams(vmem_limit_bytes=VMEM_LIMIT),
    )(pieces)


def step_body(second, col_ref, place_ref, hessian_ref, packed_ref, book_row_ref, refs):
    error_refs, refs = refs[:8], refs[8:]
    if second:
        code_refs, (near_ref, far_ref, book_col_ref), refs = refs[:8], refs[8:11], refs[11:]
    keep_ref, send_ref, eh_ref, el_ref, hh_ref, hl_ref, grad_ref, sums_ref, table_ref = refs
    q = pl.program_id(0)
    place = place_ref[0]
    col = col_ref[0]

    @pl.when(q == 0)
    def _():
        if second:
            chosen = jnp.where((book_col_ref[...] ^ place) == iota((256, 512), 1), 1.0, 0.0).astype(BF16)
            total = jnp.zeros((256, 512), F32)
            for part, ref in ((0, near_ref), (1, far_ref)):
                high, low = split(ref[...])
                here = chosen[:, part * 256 : part * 256 + 256]
                total = total + dot_nn(here, high) + dot_nn(here, low)
            table_ref[...] = total * LEARN_RATE
        for core in range(2):
            for kx in range(4):
                for kyh in range(2):
                    origin = col ^ (kx * 4 + kyh * 2 + core)
                    start = pl.multiple_of(origin * 16, 16)
                    tile_base = core * 128 + (kx * 2 + kyh) * 16

                    def column(b, carry, error_ref=error_refs[core * 4 + kx], kyh=kyh, start=start, tile_base=tile_base, code_index=core * 4 + kx):
                        for parity in range(2):
                            for c in range(2):
                                value = error_ref[kyh, b * 2 + c, parity * 16 : parity * 16 + 16, :]
                                if second:
                                    moves = []
                                    for t in range(2):
                                        code = code_refs[code_index][
                                            kyh, parity * 16 + t * 8 : parity * 16 + t * 8 + 8, pl.ds(pl.multiple_of(b * 128, 128), 128)
                                        ]
                                        tables = [
                                            jnp.broadcast_to(
                                                table_ref[pl.ds(tile_base + t * 8 + b, 1), c * 256 + k * 128 : c * 256 + k * 128 + 128],
                                                (8, 128),
                                            )
                                            for k in range(2)
                                        ]
                                        moves.append(lookup(code, *tables))
                                    value = value - jnp.concatenate(moves, axis=0)
                                high, low = split(value)
                                eh_ref[b, pl.ds(parity * 256 + start, 16), c * 128 : c * 128 + 128] = high
                                el_ref[b, pl.ds(parity * 256 + start, 16), c * 128 : c * 128 + 128] = low
                        return carry

                    lax.fori_loop(0, 8, column, 0, unroll=True)

    for j in range(8):
        for c in range(2):
            high, low = split(hessian_ref[pl.ds(c * 8 + j, 128, stride=16), :])
            hh_ref[c * 128 : c * 128 + 128, j * 128 : j * 128 + 128] = high
            hl_ref[c * 128 : c * 128 + 128, j * 128 : j * 128 + 128] = low
    for part in range(4):
        cut = slice(part * 256, part * 256 + 256)
        more = dot_nn(eh_ref[q], hh_ref[:, cut]) + dot_nn(el_ref[q], hh_ref[:, cut]) + dot_nn(eh_ref[q], hl_ref[:, cut])

        @pl.when(q == 0)
        def _():
            grad_ref[part] = more

        @pl.when(q > 0)
        def _():
            grad_ref[part] += more

    @pl.when(q == 7)
    def _():
        parting = part_pairs()
        running = jnp.where((iota((256, 128), 0) & 127) <= iota((256, 128), 1), 1.0, 0.0).astype(BF16)
        lane = iota((32, 128), 1)
        for j in range(8):
            part, cut = j // 2, slice((j % 2) * 128, (j % 2) * 128 + 128)
            both = jnp.concatenate([grad_ref[part, 0:256, cut], grad_ref[part, 256:512, cut]], axis=1)
            high, low = split(both)
            pairs = dot_nn(high, parting) + dot_nn(low, parting)
            packed = packed_ref[j]
            source = packed & 127
            counts = [(packed >> 8) & 255, packed >> 16]
            for c in range(2):
                ordered = lanes(pairs[:, c * 128 : c * 128 + 128], source)
                prefix = dot_nn(jnp.concatenate(split(ordered), axis=1), running)
                upto = []
                for count in counts:
                    value = jnp.where(count > 0, lanes(prefix, jnp.maximum(count - 1, 0)), 0.0)
                    upto.append(value.reshape(32, 8, 128).sum(axis=1))
                before = [pltpu.roll(v, 1, 1) for v in upto]
                at = c * 256
                sums_ref[j, :, at : at + 128] = 2.0 * (upto[0] - jnp.where(lane == 0, 0.0, before[0]))
                sums_ref[j, :, at + 128 : at + 256] = 2.0 * (upto[1] - jnp.where(lane == 0, before[0], before[1]))
        chosen = jnp.where((iota((512, 256), 0) ^ place) == book_row_ref[...], 1.0, 0.0).astype(BF16)
        high, low = split(sums_ref[...].reshape(256, 512))
        total = dot_nn(chosen, high) + dot_nn(chosen, low)
        keep_ref[...] = total[0:256]
        send_ref[...] = total[256:512]


def step(second, col, place, hessian, packed, book_row, *rest):
    def kernel(col_ref, place_ref, hessian_ref, packed_ref, book_row_ref, *refs):
        step_body(second, col_ref, place_ref, hessian_ref, packed_ref, book_row_ref, refs)

    half = jax.ShapeDtypeStruct((256, 512), F32)
    return pl.pallas_call(
        kernel,
        out_shape=[half, half],
        grid=(8,),
        in_specs=[in_smem(), in_smem(), pl.BlockSpec((2048, 128), lambda q: (q, 0)), whole(packed), whole(book_row)]
        + [whole(x) for x in rest],
        out_specs=[pl.BlockSpec((256, 512), lambda q: (0, 0))] * 2,
        scratch_shapes=[
            pltpu.VMEM((8, 512, 256), BF16),
            pltpu.VMEM((8, 512, 256), BF16),
            pltpu.VMEM((256, 1024), BF16),
            pltpu.VMEM((256, 1024), BF16),
            pltpu.VMEM((4, 512, 256), F32),
            pltpu.VMEM((8, 32, 512), F32),
            pltpu.VMEM((256, 512), F32),
        ],
        compiler_params=pltpu.CompilerParams(vmem_limit_bytes=VMEM_LIMIT),
    )(col, place, hessian, packed, book_row, *rest)


def last_kernel(place_ref, books_ref, near0_ref, far0_ref, near1_ref, far1_ref, out_ref):
    place = place_ref[0]
    for part, (a_ref, b_ref) in enumerate(((near0_ref, near1_ref), (far0_ref, far1_ref))):
        for k in range(4):
            start = pl.multiple_of((part * 256 + k * 64) ^ place, 64)
            for c in range(2):
                cut = (slice(k * 64, k * 64 + 64), slice(c * 256, c * 256 + 256))
                moved = LEARN_RATE * (a_ref[cut] + b_ref[cut])
                out_ref[pl.ds(start, 64), c, :] = books_ref[pl.ds(start, 64), c, :] - moved


def last(place, codebooks, *parts):
    vmem = pl.BlockSpec(memory_space=pltpu.VMEM)
    return pl.pallas_call(
        last_kernel,
        out_shape=jax.ShapeDtypeStruct((512, 2, 256), F32),
        in_specs=[pl.BlockSpec(memory_space=pltpu.SMEM)] + [vmem] * 5,
        out_specs=vmem,
    )(place, codebooks, *parts)


def sum_all(keep, send):
    half = keep + swap(send, dcore=1)
    quarter = [half[k * 64 : k * 64 + 64] for k in range(4)]
    got = [None] + [swap(quarter[k], dx=k) for k in (1, 2, 3)]
    s = (quarter[0] + got[2]) + (got[1] + got[3])
    got = [None] + [swap(s, dyl=k & 1, dyh=k >> 1) for k in (1, 2, 3)]
    s = (s + got[2]) + (got[1] + got[3])
    got = [None] + [swap(s, dz=k) for k in (1, 2, 3)]
    s = (s + got[2]) + (got[1] + got[3])
    near = jnp.concatenate([s] + [swap(s, dx=k) for k in (1, 2, 3)])
    return near, swap(near, dcore=1)


def gather_col(own):
    pair = jnp.stack([own, swap(own, dyh=1)])
    near = [pair] + [swap(pair, dx=k) for k in (1, 2, 3)]
    return near + [swap(v, dcore=1) for v in near]


def per_device(hessian, weights, codes, tile_map, codebooks):
    col = lax.axis_index("col").astype(I32)
    place = ((col & 1) * 256 + (col >> 2) * 64).reshape(1)
    col = col.reshape(1)
    rows = hessian.reshape(16384, 128)
    spread, own = make_pieces(codes, tile_map)
    pieces = lax.all_to_all(spread.reshape(128, 24, 128), BOTH, 0, 0, tiled=True)
    errors = gather_col(first(weights, own, tile_map, codebooks))
    packed = sort_codes(pieces)
    book_row = pieces[:, 16, 0:2].reshape(1, 256)
    keep, send = step(False, col, place, rows, packed, book_row, *errors)

    around = gather_col(own)
    book_col = jnp.concatenate([v[:, 32:34, 0:8] for v in around]).reshape(256, 1)
    near0, far0 = sum_all(keep, send)
    keep, send = step(True, col, place, rows, packed, book_row, *errors, *around, near0, far0, book_col)
    near1, far1 = sum_all(keep, send)
    return last(place, codebooks, near0, far0, near1, far1)


def solution(mesh):
    placed = (P("row", None, "col", None), P("col", "row"), P("col", "row"), P("col", "row"), P())
    return jax.shard_map(per_device, mesh=mesh, in_specs=placed, out_specs=P(), check_vma=False)
```

```python
import jax
import jax.numpy as jnp
from jax import lax
from jax.experimental import pallas as pl
from jax.experimental.pallas import tpu as pltpu
from jax.sharding import PartitionSpec as P

F32 = jnp.float32
BF16 = jnp.bfloat16
I32 = jnp.int32
LEARN_RATE = 0.01
BOTH = ("row", "col")
VMEM_LIMIT = 56 * 1024 * 1024
STEP_FLOPS = 18 * 10**9
SORT_FLOPS = 18 * 10**9


def partners(dx, dyh, dcore, dyl, dz):
    flip_col = dx * 4 + dyh * 2 + dcore
    flip_row = dyl * 4 + dz
    return [(i, i ^ (flip_row * 16 + flip_col)) for i in range(128)]


def swap(v, dx=0, dyh=0, dcore=0, dyl=0, dz=0):
    return lax.ppermute(v, BOTH, partners(dx, dyh, dcore, dyl, dz))


def lanes(x, index):
    return jnp.take_along_axis(x, index, axis=1, mode="promise_in_bounds")


def iota(shape, dim):
    return lax.broadcasted_iota(I32, shape, dim)


def split(x):
    high = x.astype(BF16)
    low = (x - high.astype(F32)).astype(BF16)
    return high, low


def dot_nt(a, b):
    return lax.dot_general(a, b, (((1,), (1,)), ((), ())), preferred_element_type=F32)


def dot_nn(a, b):
    return lax.dot_general(a, b, (((1,), (0,)), ((), ())), preferred_element_type=F32)


def whole(x):
    return pl.BlockSpec(x.shape, lambda *_: (0,) * x.ndim)


def in_vmem(n):
    return [pl.BlockSpec(memory_space=pltpu.VMEM)] * n


def in_smem():
    return pl.BlockSpec(memory_space=pltpu.SMEM)


def lookup(code, low_table, high_table):
    low = code & 127
    return jnp.where(code >= 128, lanes(high_table, low), lanes(low_table, low))


def part_pairs():
    lane = iota((256, 256), 1)
    return jnp.where(iota((256, 256), 0) == 2 * (lane & 127) + (lane >> 7), 1.0, 0.0).astype(BF16)


def tile_rows(start, tile, parity):
    return pl.ds(start + tile * 16 + parity, 8, stride=2)


def pieces_kernel(tile_ref, codes_ref, piece_ref, own_ref, held_ref):
    lane = iota((8, 128), 1)
    left = lane < 64
    for q in range(8):
        cut = slice(q * 128, q * 128 + 128)
        held_ref[q * 32 : q * 32 + 32, :] = codes_ref[:, cut]
        for t in range(2):
            even = held_ref[tile_rows(q * 32, t, 0), :]
            odd = held_ref[tile_rows(q * 32, t, 1), :]
            own_ref[t * 8 : t * 8 + 8, cut] = even
            own_ref[16 + t * 8 : 24 + t * 8, cut] = odd
            pair = [
                jnp.where(left, even, pltpu.roll(odd, 64, 1)),
                jnp.where(left, pltpu.roll(even, 64, 1), odd),
            ]
            for h in range(2):
                for copy in range(8):
                    piece_ref[copy, 2 * q + h, t * 8 : t * 8 + 8, :] = pair[h]
        books = jnp.where(lane == 0, tile_ref[0, q], tile_ref[1, q])
        for h in range(2):
            for copy in range(8):
                piece_ref[copy, 2 * q + h, 16:24, :] = books
    wide = iota((8, 1024), 1)
    rows = []
    for t in range(2):
        row = jnp.zeros((8, 1024), I32)
        for q in range(8):
            row = jnp.where(wide == q, tile_ref[t, q], row)
        rows.append(row)
    own_ref[32:40, :] = jnp.where(iota((8, 1024), 0) == 0, rows[0], rows[1])


def make_pieces(codes, tile_map):
    return pl.pallas_call(
        pieces_kernel,
        out_shape=[jax.ShapeDtypeStruct((8, 16, 24, 128), I32), jax.ShapeDtypeStruct((40, 1024), I32)],
        in_specs=[in_smem()] + in_vmem(1),
        out_specs=in_vmem(2),
        scratch_shapes=[pltpu.VMEM((256, 128), I32)],
    )(tile_map, codes)


def first_kernel(tile_ref, weights_ref, own_ref, books_ref, error_ref, weight_ref):
    parting = part_pairs()
    for q in range(8):
        parted = dot_nn(weights_ref[:, q * 256 : q * 256 + 256], parting)
        weight_ref[q * 64 : q * 64 + 32, :] = parted[:, 0:128]
        weight_ref[q * 64 + 32 : q * 64 + 64, :] = parted[:, 128:256]
    for q in range(8):
        for t in range(2):
            book = books_ref[tile_ref[t, q]]
            for c in range(2):
                tables = [jnp.broadcast_to(book[c : c + 1, k * 128 : k * 128 + 128], (8, 128)) for k in range(2)]
                for parity in range(2):
                    row = parity * 16 + t * 8
                    code = own_ref[row : row + 8, q * 128 : q * 128 + 128]
                    weight = weight_ref[tile_rows((q * 2 + c) * 32, t, parity), :]
                    error_ref[q * 2 + c, row : row + 8, :] = lookup(code, *tables) - weight


def first(weights, own, tile_map, codebooks):
    return pl.pallas_call(
        first_kernel,
        out_shape=jax.ShapeDtypeStruct((16, 32, 128), F32),
        in_specs=[in_smem()] + in_vmem(3),
        out_specs=in_vmem(1)[0],
        scratch_shapes=[pltpu.VMEM((512, 128), F32)],
    )(tile_map, weights, own, codebooks)


def spot(position):
    return ((position & 15) << 3) | (position >> 4)


def spot_back(lane):
    return ((lane & 7) << 4) | (lane >> 3)


def sort_block(keys):
    rows = [keys[v * 8 : v * 8 + 8, :] for v in range(16)]
    sub = iota((8, 128), 0)
    k = 2
    while k <= 128:
        j = k // 2
        while j >= 1:
            if j < 16:
                for v in range(16):
                    if v & j:
                        continue
                    a, b = rows[v], rows[v | j]
                    small, large = jnp.minimum(a, b), jnp.maximum(a, b)
                    if k < 16:
                        rising = (v & k) == 0
                        rows[v], rows[v | j] = (small, large) if rising else (large, small)
                    elif k == 128:
                        rows[v], rows[v | j] = small, large
                    else:
                        up = (sub & (k >> 4)) == 0
                        rows[v], rows[v | j] = jnp.where(up, small, large), jnp.where(up, large, small)
            else:
                step = j >> 4
                lower = (sub & step) == 0
                up = lower if k == 128 else ((sub & (k >> 4)) == 0) == lower
                for v in range(16):
                    other = jnp.where(lower, pltpu.roll(rows[v], 8 - step, 0), pltpu.roll(rows[v], step, 0))
                    rows[v] = jnp.where(up, jnp.minimum(rows[v], other), jnp.maximum(rows[v], other))
            j //= 2
        k *= 2
    return jnp.concatenate(rows, axis=0)


def sort_kernel(piece_ref, packed_ref):
    lane = iota((256, 128), 1)
    key = (piece_ref[:, 0:16, :].reshape(256, 128) * 128 + lane).astype(F32)
    halves = [sort_block(key[h * 128 : h * 128 + 128, :].T).T for h in range(2)]
    code = jnp.concatenate(halves, axis=0).astype(I32)
    counts = []
    for half in range(2):
        limit = (half * 128 + lane + 1) * 128
        count = jnp.zeros((256, 128), I32)
        for step in (64, 32, 16, 8, 4, 2, 1, 1):
            below = lanes(code, spot(count + (step - 1))) < limit
            count = jnp.where(below, count + step, count)
        counts.append(count)
    packed_ref[0] = (code & 127) | (counts[0] << 8) | (counts[1] << 16)


def sort_codes(pieces):
    return pl.pallas_call(
        sort_kernel,
        out_shape=jax.ShapeDtypeStruct((8, 256, 128), I32),
        grid=(8,),
        in_specs=[pl.BlockSpec((16, 24, 128), lambda j: (j, 0, 0))],
        out_specs=pl.BlockSpec((1, 256, 128), lambda j: (j, 0, 0)),
        compiler_params=pltpu.CompilerParams(vmem_limit_bytes=VMEM_LIMIT),
        cost_estimate=pl.CostEstimate(flops=SORT_FLOPS, bytes_accessed=3 * 1024 * 1024, transcendentals=0),
    )(pieces)


def step_body(second, col_ref, place_ref, hessian_ref, packed_ref, book_row_ref, refs):
    error_refs, refs = refs[:8], refs[8:]
    if second:
        code_refs, (near_ref, far_ref, book_col_ref), refs = refs[:8], refs[8:11], refs[11:]
    keep_ref, send_ref, left_ref, right_ref, grad_ref, sums_ref, table_ref = refs
    n = pl.program_id(0)
    place = place_ref[0]
    col = col_ref[0]
    slot, before = lax.rem(n, 2), lax.rem(n + 1, 2)

    @pl.when(n == 0)
    def _():
        left_ref[1] = jnp.zeros((512, 768), BF16)
        right_ref[1] = jnp.zeros((768, 1024), BF16)
        grad_ref[...] = jnp.zeros((4, 512, 256), F32)
        if second:
            chosen = jnp.where((book_col_ref[...] ^ place) == iota((256, 512), 1), 1.0, 0.0).astype(BF16)
            total = jnp.zeros((256, 512), F32)
            for part, ref in ((0, near_ref), (1, far_ref)):
                high, low = split(ref[...])
                here = chosen[:, part * 256 : part * 256 + 256]
                total = total + dot_nn(here, high) + dot_nn(here, low)
            table_ref[...] = (total * LEARN_RATE).reshape(8, 32, 512)

    for part in range(4):
        cut = slice(part * 256, part * 256 + 256)
        for m in range(2):
            rows = slice(m * 256, m * 256 + 256)
            grad_ref[part, rows, :] += dot_nn(left_ref[before, rows, :], right_ref[before, :, cut])

    b = jnp.minimum(n, 7)
    for core in range(2):
        for kx in range(4):
            which = core * 4 + kx
            for kyh in range(2):
                origin = col ^ (kx * 4 + kyh * 2 + core)
                start = pl.multiple_of(origin * 16, 16)
                base = core * 16 + (kx * 2 + kyh) * 2
                for c in range(2):
                    if second:
                        tables = [
                            [
                                jnp.broadcast_to(table_ref[b, base + t : base + t + 1, (c * 2 + k) * 128 : (c * 2 + k) * 128 + 128], (8, 128))
                                for k in range(2)
                            ]
                            for t in range(2)
                        ]
                    for parity in range(2):
                        value = error_refs[which][kyh, c, parity * 16 : parity * 16 + 16, :]
                        if second:
                            moves = [
                                lookup(code_refs[which][kyh, parity * 16 + t * 8 : parity * 16 + t * 8 + 8, :], *tables[t])
                                for t in range(2)
                            ]
                            value = value - jnp.concatenate(moves, axis=0)
                        high, low = split(value)
                        rows = pl.ds(parity * 256 + start, 16)
                        left_ref[slot, rows, c * 128 : c * 128 + 128] = high
                        left_ref[slot, rows, 256 + c * 128 : 256 + c * 128 + 128] = low
                        left_ref[slot, rows, 512 + c * 128 : 512 + c * 128 + 128] = high
    for j in range(8):
        for c in range(2):
            high, low = split(hessian_ref[pl.ds(c * 8 + j, 128, stride=16), :])
            cut = slice(j * 128, j * 128 + 128)
            right_ref[slot, c * 128 : c * 128 + 128, cut] = high
            right_ref[slot, 256 + c * 128 : 256 + c * 128 + 128, cut] = high
            right_ref[slot, 512 + c * 128 : 512 + c * 128 + 128, cut] = low

    @pl.when(n == 8)
    def _():
        parting = part_pairs()
        running = jnp.where(spot_back(iota((256, 128), 0) & 127) <= iota((256, 128), 1), 1.0, 0.0).astype(BF16)
        lane = iota((32, 128), 1)
        for j in range(8):
            part, cut = j // 2, slice((j % 2) * 128, (j % 2) * 128 + 128)
            both = jnp.concatenate([grad_ref[part, 0:256, cut], grad_ref[part, 256:512, cut]], axis=1)
            high, low = split(both)
            pairs = dot_nn(high, parting) + dot_nn(low, parting)
            packed = packed_ref[j]
            source = packed & 127
            counts = [(packed >> 8) & 255, packed >> 16]
            for c in range(2):
                ordered = lanes(pairs[:, c * 128 : c * 128 + 128], source)
                prefix = dot_nn(jnp.concatenate(split(ordered), axis=1), running)
                upto = []
                for count in counts:
                    value = jnp.where(count > 0, lanes(prefix, jnp.maximum(count - 1, 0)), 0.0)
                    upto.append(value.reshape(32, 8, 128).sum(axis=1))
                earlier = [pltpu.roll(v, 1, 1) for v in upto]
                at = c * 256
                sums_ref[j, :, at : at + 128] = 2.0 * (upto[0] - jnp.where(lane == 0, 0.0, earlier[0]))
                sums_ref[j, :, at + 128 : at + 256] = 2.0 * (upto[1] - jnp.where(lane == 0, earlier[0], earlier[1]))
        chosen = jnp.where((iota((512, 256), 0) ^ place) == book_row_ref[...], 1.0, 0.0).astype(BF16)
        high, low = split(sums_ref[...].reshape(256, 512))
        total = dot_nn(chosen, high) + dot_nn(chosen, low)
        keep_ref[...] = total[0:256]
        send_ref[...] = total[256:512]


def step(second, col, place, hessian, packed, book_row, *rest):
    def kernel(col_ref, place_ref, hessian_ref, packed_ref, book_row_ref, *refs):
        step_body(second, col_ref, place_ref, hessian_ref, packed_ref, book_row_ref, refs)

    half = jax.ShapeDtypeStruct((256, 512), F32)
    errors = [pl.BlockSpec((2, 2, 32, 128), lambda n: (0, jnp.minimum(n, 7), 0, 0))] * 8
    codes = [pl.BlockSpec((2, 40, 128), lambda n: (0, 0, jnp.minimum(n, 7)))] * 8
    return pl.pallas_call(
        kernel,
        out_shape=[half, half],
        grid=(9,),
        in_specs=[
            in_smem(),
            in_smem(),
            pl.BlockSpec((2048, 128), lambda n: (jnp.minimum(n, 7), 0)),
            whole(packed),
            whole(book_row),
        ]
        + errors
        + (codes + [whole(x) for x in rest[16:]] if second else []),
        out_specs=[pl.BlockSpec((256, 512), lambda n: (0, 0))] * 2,
        scratch_shapes=[
            pltpu.VMEM((2, 512, 768), BF16),
            pltpu.VMEM((2, 768, 1024), BF16),
            pltpu.VMEM((4, 512, 256), F32),
            pltpu.VMEM((8, 32, 512), F32),
            pltpu.VMEM((8, 32, 512), F32),
        ],
        compiler_params=pltpu.CompilerParams(vmem_limit_bytes=VMEM_LIMIT),
        cost_estimate=pl.CostEstimate(flops=STEP_FLOPS, bytes_accessed=16 * 1024 * 1024, transcendentals=0),
    )(col, place, hessian, packed, book_row, *rest)


def last_kernel(place_ref, books_ref, near0_ref, far0_ref, near1_ref, far1_ref, out_ref):
    place = place_ref[0]
    for part, (a_ref, b_ref) in enumerate(((near0_ref, near1_ref), (far0_ref, far1_ref))):
        for k in range(4):
            start = pl.multiple_of((part * 256 + k * 64) ^ place, 64)
            for c in range(2):
                cut = (slice(k * 64, k * 64 + 64), slice(c * 256, c * 256 + 256))
                moved = LEARN_RATE * (a_ref[cut] + b_ref[cut])
                out_ref[pl.ds(start, 64), c, :] = books_ref[pl.ds(start, 64), c, :] - moved


def last(place, codebooks, *parts):
    vmem = pl.BlockSpec(memory_space=pltpu.VMEM)
    return pl.pallas_call(
        last_kernel,
        out_shape=jax.ShapeDtypeStruct((512, 2, 256), F32),
        in_specs=[pl.BlockSpec(memory_space=pltpu.SMEM)] + [vmem] * 5,
        out_specs=vmem,
    )(place, codebooks, *parts)


def sum_all(keep, send):
    half = keep + swap(send, dcore=1)
    quarter = [half[k * 64 : k * 64 + 64] for k in range(4)]
    got = [None] + [swap(quarter[k], dx=k) for k in (1, 2, 3)]
    s = (quarter[0] + got[2]) + (got[1] + got[3])
    got = [None] + [swap(s, dyl=k & 1, dyh=k >> 1) for k in (1, 2, 3)]
    s = (s + got[2]) + (got[1] + got[3])
    got = [None] + [swap(s, dz=k) for k in (1, 2, 3)]
    s = (s + got[2]) + (got[1] + got[3])
    near = jnp.concatenate([s] + [swap(s, dx=k) for k in (1, 2, 3)])
    return near, swap(near, dcore=1)


def hold(*values):
    return lax.optimization_barrier(values)


def pair_up(own):
    return jnp.stack([own, swap(own, dyh=1)])


def over_x(pair):
    return [pair] + [swap(pair, dx=k) for k in (1, 2, 3)]


def both_cores(near):
    return list(near) + [swap(v, dcore=1) for v in near]


def per_device(hessian, weights, codes, tile_map, codebooks):
    col = lax.axis_index("col").astype(I32)
    place = ((col & 1) * 256 + (col >> 2) * 64).reshape(1)
    col = col.reshape(1)
    rows = hessian.reshape(16384, 128)
    spread, own = make_pieces(codes, tile_map)
    pieces = lax.all_to_all(spread.reshape(128, 24, 128), BOTH, 0, 0, tiled=True)
    error_pair, code_pair = pair_up(first(weights, own, tile_map, codebooks)), pair_up(own)
    pieces, error_pair, code_pair = hold(pieces, error_pair, code_pair)
    packed = sort_codes(pieces)
    book_row = pieces[:, 16, 0:2].reshape(1, 256)
    packed, book_row, code_pair, *errors = hold(packed, book_row, code_pair, *over_x(error_pair))
    errors = both_cores(errors)
    keep, send = step(False, col, place, rows, packed, book_row, *errors)
    keep, send, *around = hold(keep, send, *over_x(code_pair))
    around = both_cores(around)
    book_col = jnp.concatenate([v[:, 32:34, 0:8] for v in around]).reshape(32, 8).T.reshape(256, 1)
    near0, far0 = sum_all(keep, send)
    keep, send = step(True, col, place, rows, packed, book_row, *errors, *around, near0, far0, book_col)
    near1, far1 = sum_all(keep, send)
    return last(place, codebooks, near0, far0, near1, far1)


def solution(mesh):
    placed = (P("row", None, "col", None), P("col", "row"), P("col", "row"), P("col", "row"), P())
    return jax.shard_map(per_device, mesh=mesh, in_specs=placed, out_specs=P(), check_vma=False)
```

```python
import jax
import jax.numpy as jnp
from jax import lax
from jax.experimental import pallas as pl
from jax.experimental.pallas import tpu as pltpu
from jax.sharding import PartitionSpec as P

F32 = jnp.float32
BF16 = jnp.bfloat16
I32 = jnp.int32
LEARN_RATE = 0.01
BOTH = ("row", "col")
VMEM_LIMIT = 56 * 1024 * 1024
STEP_FLOPS = 18 * 10**9
SORT_FLOPS = 5 * 10**9
SPLIT_FLOPS = 9 * 10**9


def partners(dx, dyh, dcore, dyl, dz):
    flip_col = dx * 4 + dyh * 2 + dcore
    flip_row = dyl * 4 + dz
    return [(i, i ^ (flip_row * 16 + flip_col)) for i in range(128)]


def swap(v, dx=0, dyh=0, dcore=0, dyl=0, dz=0):
    return lax.ppermute(v, BOTH, partners(dx, dyh, dcore, dyl, dz))


def lanes(x, index):
    return jnp.take_along_axis(x, index, axis=1, mode="promise_in_bounds")


def iota(shape, dim):
    return lax.broadcasted_iota(I32, shape, dim)


def split(x):
    high = x.astype(BF16)
    low = (x - high.astype(F32)).astype(BF16)
    return high, low


def dot_nt(a, b):
    return lax.dot_general(a, b, (((1,), (1,)), ((), ())), preferred_element_type=F32)


def dot_nn(a, b):
    return lax.dot_general(a, b, (((1,), (0,)), ((), ())), preferred_element_type=F32)


def whole(x):
    return pl.BlockSpec(x.shape, lambda *_: (0,) * x.ndim)


def in_vmem(n):
    return [pl.BlockSpec(memory_space=pltpu.VMEM)] * n


def in_smem():
    return pl.BlockSpec(memory_space=pltpu.SMEM)


def lookup(code, low_table, high_table):
    low = code & 127
    return jnp.where(code >= 128, lanes(high_table, low), lanes(low_table, low))


def part_pairs():
    lane = iota((256, 256), 1)
    return jnp.where(iota((256, 256), 0) == 2 * (lane & 127) + (lane >> 7), 1.0, 0.0).astype(BF16)


def tile_rows(start, tile, parity):
    return pl.ds(start + tile * 16 + parity, 8, stride=2)


def pieces_kernel(tile_ref, codes_ref, piece_ref, own_ref, held_ref):
    lane = iota((8, 128), 1)
    left = lane < 64
    for q in range(8):
        cut = slice(q * 128, q * 128 + 128)
        held_ref[q * 32 : q * 32 + 32, :] = codes_ref[:, cut]
        for t in range(2):
            even = held_ref[tile_rows(q * 32, t, 0), :]
            odd = held_ref[tile_rows(q * 32, t, 1), :]
            own_ref[t * 8 : t * 8 + 8, cut] = even
            own_ref[16 + t * 8 : 24 + t * 8, cut] = odd
            pair = [
                jnp.where(left, even, pltpu.roll(odd, 64, 1)),
                jnp.where(left, pltpu.roll(even, 64, 1), odd),
            ]
            for h in range(2):
                piece_ref[2 * q + h, t * 8 : t * 8 + 8, :] = pair[h]
        books = jnp.where(lane == 0, tile_ref[0, q], tile_ref[1, q])
        for h in range(2):
            piece_ref[2 * q + h, 16:24, :] = books
    wide = iota((8, 1024), 1)
    rows = []
    for t in range(2):
        row = jnp.zeros((8, 1024), I32)
        for q in range(8):
            row = jnp.where(wide == q, tile_ref[t, q], row)
        rows.append(row)
    own_ref[32:40, :] = jnp.where(iota((8, 1024), 0) == 0, rows[0], rows[1])


def make_pieces(codes, tile_map):
    return pl.pallas_call(
        pieces_kernel,
        out_shape=[jax.ShapeDtypeStruct((16, 24, 128), I32), jax.ShapeDtypeStruct((40, 1024), I32)],
        in_specs=[in_smem()] + in_vmem(1),
        out_specs=in_vmem(2),
        scratch_shapes=[pltpu.VMEM((256, 128), I32)],
    )(tile_map, codes)


def first_kernel(tile_ref, weights_ref, own_ref, books_ref, error_ref, weight_ref):
    parting = part_pairs()
    for q in range(8):
        parted = dot_nn(weights_ref[:, q * 256 : q * 256 + 256], parting)
        weight_ref[q * 64 : q * 64 + 32, :] = parted[:, 0:128]
        weight_ref[q * 64 + 32 : q * 64 + 64, :] = parted[:, 128:256]
    for q in range(8):
        for t in range(2):
            book = books_ref[tile_ref[t, q]]
            for c in range(2):
                tables = [jnp.broadcast_to(book[c : c + 1, k * 128 : k * 128 + 128], (8, 128)) for k in range(2)]
                for parity in range(2):
                    row = parity * 16 + t * 8
                    code = own_ref[row : row + 8, q * 128 : q * 128 + 128]
                    weight = weight_ref[tile_rows((q * 2 + c) * 32, t, parity), :]
                    error_ref[q * 2 + c, row : row + 8, :] = lookup(code, *tables) - weight


def first(weights, own, tile_map, codebooks):
    return pl.pallas_call(
        first_kernel,
        out_shape=jax.ShapeDtypeStruct((16, 32, 128), F32),
        in_specs=[in_smem()] + in_vmem(3),
        out_specs=in_vmem(1)[0],
        scratch_shapes=[pltpu.VMEM((512, 128), F32)],
    )(tile_map, weights, own, codebooks)


def spot(position):
    return ((position & 15) << 3) | (position >> 4)


def spot_back(lane):
    return ((lane & 7) << 4) | (lane >> 3)


def sort_block(keys):
    rows = [keys[v * 8 : v * 8 + 8, :] for v in range(16)]
    sub = iota((8, 128), 0)
    k = 2
    while k <= 128:
        j = k // 2
        while j >= 1:
            if j < 16:
                for v in range(16):
                    if v & j:
                        continue
                    a, b = rows[v], rows[v | j]
                    small, large = jnp.minimum(a, b), jnp.maximum(a, b)
                    if k < 16:
                        rising = (v & k) == 0
                        rows[v], rows[v | j] = (small, large) if rising else (large, small)
                    elif k == 128:
                        rows[v], rows[v | j] = small, large
                    else:
                        up = (sub & (k >> 4)) == 0
                        rows[v], rows[v | j] = jnp.where(up, small, large), jnp.where(up, large, small)
            else:
                step = j >> 4
                lower = (sub & step) == 0
                up = lower if k == 128 else ((sub & (k >> 4)) == 0) == lower
                for v in range(16):
                    other = jnp.where(lower, pltpu.roll(rows[v], 8 - step, 0), pltpu.roll(rows[v], step, 0))
                    rows[v] = jnp.where(up, jnp.minimum(rows[v], other), jnp.maximum(rows[v], other))
            j //= 2
        k *= 2
    return jnp.concatenate(rows, axis=0)


def sort_kernel(piece_ref, packed_ref):
    lane = iota((256, 128), 1)
    key = (piece_ref[0, :, 0:16, :].reshape(256, 128) * 128 + lane).astype(F32)
    halves = [sort_block(key[h * 128 : h * 128 + 128, :].T).T for h in range(2)]
    code = jnp.concatenate(halves, axis=0).astype(I32)
    counts = []
    for half in range(2):
        limit = (half * 128 + lane + 1) * 128
        count = jnp.zeros((256, 128), I32)
        for step in (64, 32, 16, 8, 4, 2, 1, 1):
            below = lanes(code, spot(count + (step - 1))) < limit
            count = jnp.where(below, count + step, count)
        counts.append(count)
    packed_ref[0] = (code & 127) | (counts[0] << 8) | (counts[1] << 16)


def sort_codes(pieces):
    return pl.pallas_call(
        sort_kernel,
        out_shape=jax.ShapeDtypeStruct((2, 256, 128), I32),
        grid=(2,),
        in_specs=[pl.BlockSpec((1, 16, 24, 128), lambda j: (j, 0, 0, 0))],
        out_specs=pl.BlockSpec((1, 256, 128), lambda j: (j, 0, 0)),
        compiler_params=pltpu.CompilerParams(vmem_limit_bytes=VMEM_LIMIT),
        cost_estimate=pl.CostEstimate(flops=SORT_FLOPS, bytes_accessed=1024 * 1024, transcendentals=0),
    )(pieces)


def split_kernel(hessian_ref, right_ref):
    for j in range(8):
        for c in range(2):
            high, low = split(hessian_ref[pl.ds(c * 8 + j, 128, stride=16), :])
            cut = slice(j * 128, j * 128 + 128)
            right_ref[0, c * 128 : c * 128 + 128, cut] = high
            right_ref[0, 256 + c * 128 : 256 + c * 128 + 128, cut] = high
            right_ref[0, 512 + c * 128 : 512 + c * 128 + 128, cut] = low


def split_hessian(rows):
    return pl.pallas_call(
        split_kernel,
        out_shape=jax.ShapeDtypeStruct((8, 768, 1024), BF16),
        grid=(8,),
        in_specs=[pl.BlockSpec((2048, 128), lambda q: (q, 0))],
        out_specs=pl.BlockSpec((1, 768, 1024), lambda q: (q, 0, 0)),
        compiler_params=pltpu.CompilerParams(vmem_limit_bytes=VMEM_LIMIT),
        cost_estimate=pl.CostEstimate(flops=SPLIT_FLOPS, bytes_accessed=20 * 1024 * 1024, transcendentals=0),
    )(rows)


def step_body(second, where_ref, packed_refs, rights, book_row_ref, refs):
    error_refs, refs = (refs[:8], refs[8:16]), refs[16:]
    if second:
        code_refs, refs = (refs[:8], refs[8:16]), refs[16:]
        (near_ref, far_ref, book_col_ref), refs = refs[:3], refs[3:]
    keep_ref, send_ref, left0_ref, left1_ref, grad_ref, sums_ref, table_ref = refs
    n = pl.program_id(0)
    row, col, place = where_ref[0], where_ref[1], where_ref[2]

    def multiply(left_ref, right_ref):
        for part in range(4):
            for m in range(2):
                rows = slice(m * 256, m * 256 + 256)
                more = dot_nn(left_ref[rows, :], right_ref[0, :, part * 256 : part * 256 + 256])
                grad_ref[2 * part, rows, :] += more[:, 0:128]
                grad_ref[2 * part + 1, rows, :] += more[:, 128:256]

    def prepare(half, left_ref):
        b = jnp.minimum(2 * n + half, 7)
        for core in range(2):
            for kx in range(4):
                which = core * 4 + kx
                for kyh in range(2):
                    start = pl.multiple_of((col ^ (kx * 4 + kyh * 2 + core)) * 16, 16)
                    base = core * 16 + (kx * 2 + kyh) * 2
                    for c in range(2):
                        if second:
                            tables = [
                                [
                                    jnp.broadcast_to(table_ref[b, base + t : base + t + 1, (c * 2 + k) * 128 : (c * 2 + k) * 128 + 128], (8, 128))
                                    for k in range(2)
                                ]
                                for t in range(2)
                            ]
                        for parity in range(2):
                            value = error_refs[half][which][kyh, c, parity * 16 : parity * 16 + 16, :]
                            if second:
                                moves = [
                                    lookup(code_refs[half][which][kyh, parity * 16 + t * 8 : parity * 16 + t * 8 + 8, :], *tables[t])
                                    for t in range(2)
                                ]
                                value = value - jnp.concatenate(moves, axis=0)
                            high, low = split(value)
                            rows = pl.ds(parity * 256 + start, 16)
                            left_ref[rows, c * 128 : c * 128 + 128] = high
                            left_ref[rows, 256 + c * 128 : 256 + c * 128 + 128] = low
                            left_ref[rows, 512 + c * 128 : 512 + c * 128 + 128] = high

    @pl.when(n == 0)
    def _():
        left1_ref[...] = jnp.zeros((512, 768), BF16)
        grad_ref[...] = jnp.zeros((8, 512, 128), F32)
        if second:
            chosen = jnp.where((book_col_ref[...] ^ place) == iota((256, 512), 1), 1.0, 0.0).astype(BF16)
            total = jnp.zeros((256, 512), F32)
            for part, ref in ((0, near_ref), (1, far_ref)):
                high, low = split(ref[...])
                here = chosen[:, part * 256 : part * 256 + 256]
                total = total + dot_nn(here, high) + dot_nn(here, low)
            table_ref[...] = (total * LEARN_RATE).reshape(8, 32, 512)

    prepare(0, left0_ref)
    multiply(left1_ref, rights[0])

    @pl.when(n < 4)
    def _():
        prepare(1, left1_ref)
        multiply(left0_ref, rights[1])

    @pl.when(n == 4)
    def _():
        parting = part_pairs()
        running = jnp.where(spot_back(iota((256, 128), 0) & 127) <= iota((256, 128), 1), 1.0, 0.0).astype(BF16)
        lane = iota((32, 128), 1)
        for kz in range(4):
            for dyl in range(2):
                j = row ^ (dyl * 4 + kz)
                at = kz * 2 + dyl
                both = jnp.concatenate([grad_ref[j, 0:256, :], grad_ref[j, 256:512, :]], axis=1)
                high, low = split(both)
                pairs = dot_nn(high, parting) + dot_nn(low, parting)
                packed = packed_refs[kz][dyl]
                source = packed & 127
                counts = [(packed >> 8) & 255, packed >> 16]
                for c in range(2):
                    ordered = lanes(pairs[:, c * 128 : c * 128 + 128], source)
                    prefix = dot_nn(jnp.concatenate(split(ordered), axis=1), running)
                    upto = []
                    for count in counts:
                        value = jnp.where(count > 0, lanes(prefix, jnp.maximum(count - 1, 0)), 0.0)
                        upto.append(value.reshape(32, 8, 128).sum(axis=1))
                    earlier = [pltpu.roll(v, 1, 1) for v in upto]
                    low_sums = 2.0 * (upto[0] - jnp.where(lane == 0, 0.0, earlier[0]))
                    high_sums = 2.0 * (upto[1] - jnp.where(lane == 0, earlier[0], earlier[1]))
                    sums_ref[at, :, c * 256 : c * 256 + 128] = low_sums
                    sums_ref[at, :, c * 256 + 128 : c * 256 + 256] = high_sums
        chosen = jnp.where((iota((512, 256), 0) ^ place) == book_row_ref[...], 1.0, 0.0).astype(BF16)
        high, low = split(sums_ref[...].reshape(256, 512))
        total = dot_nn(chosen, high) + dot_nn(chosen, low)
        keep_ref[...] = total[0:256]
        send_ref[...] = total[256:512]


def step(second, place, packed, right, book_row, errors, codes, rest):
    def kernel(where_ref, *refs):
        step_body(second, where_ref, refs[0:4], refs[4:6], refs[6], refs[7:])

    def tile_column(half):
        return lambda n: jnp.clip(2 * n + half, 0, 7)

    right_specs, error_specs, code_specs = [], [], []
    for half in (-1, 0):
        right_specs.append(pl.BlockSpec((1, 768, 1024), lambda n, f=tile_column(half): (f(n), 0, 0)))
    for half in (0, 1):
        error_specs += [pl.BlockSpec((2, 2, 32, 128), lambda n, f=tile_column(half): (0, f(n), 0, 0))] * 8
        code_specs += [pl.BlockSpec((2, 40, 128), lambda n, f=tile_column(half): (0, 0, f(n)))] * 8
    half = jax.ShapeDtypeStruct((256, 512), F32)
    return pl.pallas_call(
        kernel,
        out_shape=[half, half],
        grid=(5,),
        in_specs=[in_smem()]
        + [whole(x) for x in packed]
        + right_specs
        + [whole(book_row)]
        + error_specs
        + (code_specs if second else [])
        + [whole(x) for x in rest],
        out_specs=[pl.BlockSpec((256, 512), lambda n: (0, 0))] * 2,
        scratch_shapes=[
            pltpu.VMEM((512, 768), BF16),
            pltpu.VMEM((512, 768), BF16),
            pltpu.VMEM((8, 512, 128), F32),
            pltpu.VMEM((8, 32, 512), F32),
            pltpu.VMEM((8, 32, 512), F32),
        ],
        compiler_params=pltpu.CompilerParams(vmem_limit_bytes=VMEM_LIMIT),
        cost_estimate=pl.CostEstimate(flops=STEP_FLOPS, bytes_accessed=16 * 1024 * 1024, transcendentals=0),
    )(place, *packed, right, right, book_row, *errors, *errors, *codes, *codes, *rest)


def last_kernel(place_ref, books_ref, near0_ref, far0_ref, near1_ref, far1_ref, out_ref):
    place = place_ref[0]
    for part, (a_ref, b_ref) in enumerate(((near0_ref, near1_ref), (far0_ref, far1_ref))):
        for k in range(4):
            start = pl.multiple_of((part * 256 + k * 64) ^ place, 64)
            for c in range(2):
                cut = (slice(k * 64, k * 64 + 64), slice(c * 256, c * 256 + 256))
                moved = LEARN_RATE * (a_ref[cut] + b_ref[cut])
                out_ref[pl.ds(start, 64), c, :] = books_ref[pl.ds(start, 64), c, :] - moved


def last(place, codebooks, *parts):
    vmem = pl.BlockSpec(memory_space=pltpu.VMEM)
    return pl.pallas_call(
        last_kernel,
        out_shape=jax.ShapeDtypeStruct((512, 2, 256), F32),
        in_specs=[pl.BlockSpec(memory_space=pltpu.SMEM)] + [vmem] * 5,
        out_specs=vmem,
    )(place, codebooks, *parts)


def sum_all(keep, send):
    half = keep + swap(send, dcore=1)
    quarter = [half[k * 64 : k * 64 + 64] for k in range(4)]
    got = [None] + [swap(quarter[k], dx=k) for k in (1, 2, 3)]
    s = (quarter[0] + got[2]) + (got[1] + got[3])
    got = [None] + [swap(s, dyl=k & 1, dyh=k >> 1) for k in (1, 2, 3)]
    s = (s + got[2]) + (got[1] + got[3])
    got = [None] + [swap(s, dz=k) for k in (1, 2, 3)]
    s = (s + got[2]) + (got[1] + got[3])
    near = jnp.concatenate([s] + [swap(s, dx=k) for k in (1, 2, 3)])
    return near, swap(near, dcore=1)


def hold(*values):
    return lax.optimization_barrier(values)


def pair_up(own):
    return jnp.stack([own, swap(own, dyh=1)])


def over_x(pair):
    return [pair] + [swap(pair, dx=k) for k in (1, 2, 3)]


def both_cores(near):
    return list(near) + [swap(v, dcore=1) for v in near]


def per_device(hessian, weights, codes, tile_map, codebooks):
    row, col = lax.axis_index("row").astype(I32), lax.axis_index("col").astype(I32)
    place = (col & 1) * 256 + (col >> 2) * 64
    where = jnp.stack([row, col, place])
    place = place.reshape(1)
    pieces, own = make_pieces(codes, tile_map)
    pieces = lax.all_to_all(pieces, "col", 0, 0, tiled=True)
    error_pair = pair_up(first(weights, own, tile_map, codebooks))
    right = split_hessian(hessian.reshape(16384, 128))
    pieces, right, error_pair, own = hold(pieces, right, error_pair, own)

    errors = over_x(error_pair)
    piece_pair = jnp.stack([pieces, swap(pieces, dyl=1)])
    pieces = [piece_pair] + [swap(piece_pair, dz=k) for k in (1, 2, 3)]
    code_pair = pair_up(own)
    packed = [sort_codes(v) for v in pieces]
    book_row = jnp.concatenate([v[:, :, 16, 0:2] for v in pieces]).reshape(1, 256)
    held = hold(book_row, code_pair, *packed, *errors)
    book_row, code_pair, packed, errors = held[0], held[1], held[2:6], held[6:]
    errors = both_cores(errors)
    keep, send = step(False, where, packed, right, book_row, errors, [], [])
    keep, send, *around = hold(keep, send, *over_x(code_pair))
    around = both_cores(around)
    book_col = jnp.concatenate([v[:, 32:34, 0:8] for v in around]).reshape(32, 8).T.reshape(256, 1)
    near0, far0 = sum_all(keep, send)
    keep, send = step(True, where, packed, right, book_row, errors, around, [near0, far0, book_col])
    near1, far1 = sum_all(keep, send)
    return last(place, codebooks, near0, far0, near1, far1)


def solution(mesh):
    placed = (P("row", None, "col", None), P("col", "row"), P("col", "row"), P("col", "row"), P())
    return jax.shard_map(per_device, mesh=mesh, in_specs=placed, out_specs=P(), check_vma=False)
```

```python
import jax
import jax.numpy as jnp
from jax import lax
from jax.experimental import pallas as pl
from jax.experimental.pallas import tpu as pltpu
from jax.sharding import PartitionSpec as P

F32 = jnp.float32
BF16 = jnp.bfloat16
I32 = jnp.int32
LEARN_RATE = 0.01
BOTH = ("row", "col")
VMEM_LIMIT = 56 * 1024 * 1024
STEP_FLOPS = 18 * 10**9
SORT_FLOPS = 5 * 10**9
SPLIT_FLOPS = 9 * 10**9


def partners(dx, dyh, dcore, dyl, dz):
    flip_col = dx * 4 + dyh * 2 + dcore
    flip_row = dyl * 4 + dz
    return [(i, i ^ (flip_row * 16 + flip_col)) for i in range(128)]


def swap(v, dx=0, dyh=0, dcore=0, dyl=0, dz=0):
    return lax.ppermute(v, BOTH, partners(dx, dyh, dcore, dyl, dz))


def lanes(x, index):
    return jnp.take_along_axis(x, index, axis=1, mode="promise_in_bounds")


def iota(shape, dim):
    return lax.broadcasted_iota(I32, shape, dim)


def split(x):
    high = x.astype(BF16)
    low = (x - high.astype(F32)).astype(BF16)
    return high, low


def dot_nt(a, b):
    return lax.dot_general(a, b, (((1,), (1,)), ((), ())), preferred_element_type=F32)


def dot_nn(a, b):
    return lax.dot_general(a, b, (((1,), (0,)), ((), ())), preferred_element_type=F32)


def whole(x):
    return pl.BlockSpec(x.shape, lambda *_: (0,) * x.ndim)


def in_vmem(n):
    return [pl.BlockSpec(memory_space=pltpu.VMEM)] * n


def in_smem():
    return pl.BlockSpec(memory_space=pltpu.SMEM)


def lookup(code, low_table, high_table):
    low = code & 127
    return jnp.where(code >= 128, lanes(high_table, low), lanes(low_table, low))


def part_pairs():
    lane = iota((256, 256), 1)
    return jnp.where(iota((256, 256), 0) == 2 * (lane & 127) + (lane >> 7), 1.0, 0.0).astype(BF16)


def tile_rows(start, tile, parity):
    return pl.ds(start + tile * 16 + parity, 8, stride=2)


def pieces_kernel(tile_ref, codes_ref, piece_ref, own_ref, held_ref):
    lane = iota((8, 128), 1)
    left = lane < 64
    for q in range(8):
        cut = slice(q * 128, q * 128 + 128)
        held_ref[q * 32 : q * 32 + 32, :] = codes_ref[:, cut]
        for t in range(2):
            even = held_ref[tile_rows(q * 32, t, 0), :]
            odd = held_ref[tile_rows(q * 32, t, 1), :]
            own_ref[t * 8 : t * 8 + 8, cut] = even
            own_ref[16 + t * 8 : 24 + t * 8, cut] = odd
            pair = [
                jnp.where(left, even, pltpu.roll(odd, 64, 1)),
                jnp.where(left, pltpu.roll(even, 64, 1), odd),
            ]
            for h in range(2):
                piece_ref[2 * q + h, t * 8 : t * 8 + 8, :] = pair[h]
        books = jnp.where(lane == 0, tile_ref[0, q], tile_ref[1, q])
        for h in range(2):
            piece_ref[2 * q + h, 16:24, :] = books
    wide = iota((8, 1024), 1)
    rows = []
    for t in range(2):
        row = jnp.zeros((8, 1024), I32)
        for q in range(8):
            row = jnp.where(wide == q, tile_ref[t, q], row)
        rows.append(row)
    own_ref[32:40, :] = jnp.where(iota((8, 1024), 0) == 0, rows[0], rows[1])


def make_pieces(codes, tile_map):
    return pl.pallas_call(
        pieces_kernel,
        out_shape=[jax.ShapeDtypeStruct((16, 24, 128), I32), jax.ShapeDtypeStruct((40, 1024), I32)],
        in_specs=[in_smem()] + in_vmem(1),
        out_specs=in_vmem(2),
        scratch_shapes=[pltpu.VMEM((256, 128), I32)],
    )(tile_map, codes)


def first_kernel(tile_ref, weights_ref, own_ref, books_ref, error_ref, weight_ref):
    parting = part_pairs()
    for q in range(8):
        parted = dot_nn(weights_ref[:, q * 256 : q * 256 + 256], parting)
        weight_ref[q * 64 : q * 64 + 32, :] = parted[:, 0:128]
        weight_ref[q * 64 + 32 : q * 64 + 64, :] = parted[:, 128:256]
    for q in range(8):
        for t in range(2):
            book = books_ref[tile_ref[t, q]]
            for c in range(2):
                tables = [jnp.broadcast_to(book[c : c + 1, k * 128 : k * 128 + 128], (8, 128)) for k in range(2)]
                for parity in range(2):
                    row = parity * 16 + t * 8
                    code = own_ref[row : row + 8, q * 128 : q * 128 + 128]
                    weight = weight_ref[tile_rows((q * 2 + c) * 32, t, parity), :]
                    error_ref[q * 2 + c, row : row + 8, :] = lookup(code, *tables) - weight


def first(weights, own, tile_map, codebooks):
    return pl.pallas_call(
        first_kernel,
        out_shape=jax.ShapeDtypeStruct((16, 32, 128), F32),
        in_specs=[in_smem()] + in_vmem(3),
        out_specs=in_vmem(1)[0],
        scratch_shapes=[pltpu.VMEM((512, 128), F32)],
    )(tile_map, weights, own, codebooks)


def spot(position):
    return ((position & 15) << 3) | (position >> 4)


def spot_back(lane):
    return ((lane & 7) << 4) | (lane >> 3)


def sort_block(keys):
    rows = [keys[v * 8 : v * 8 + 8, :] for v in range(16)]
    sub = iota((8, 128), 0)
    k = 2
    while k <= 128:
        j = k // 2
        while j >= 1:
            if j < 16:
                for v in range(16):
                    if v & j:
                        continue
                    a, b = rows[v], rows[v | j]
                    small, large = jnp.minimum(a, b), jnp.maximum(a, b)
                    if k < 16:
                        rising = (v & k) == 0
                        rows[v], rows[v | j] = (small, large) if rising else (large, small)
                    elif k == 128:
                        rows[v], rows[v | j] = small, large
                    else:
                        up = (sub & (k >> 4)) == 0
                        rows[v], rows[v | j] = jnp.where(up, small, large), jnp.where(up, large, small)
            else:
                step = j >> 4
                lower = (sub & step) == 0
                up = lower if k == 128 else ((sub & (k >> 4)) == 0) == lower
                for v in range(16):
                    other = jnp.where(lower, pltpu.roll(rows[v], 8 - step, 0), pltpu.roll(rows[v], step, 0))
                    rows[v] = jnp.where(up, jnp.minimum(rows[v], other), jnp.maximum(rows[v], other))
            j //= 2
        k *= 2
    return jnp.concatenate(rows, axis=0)


def sort_kernel(*refs):
    lane = iota((256, 128), 1)
    for piece_ref, packed_ref in zip(refs[: len(refs) // 2], refs[len(refs) // 2 :]):
        key = (piece_ref[0, :, 0:16, :].reshape(256, 128) * 128 + lane).astype(F32)
        halves = [sort_block(key[h * 128 : h * 128 + 128, :].T).T for h in range(2)]
        code = jnp.concatenate(halves, axis=0).astype(I32)
        counts = []
        for half in range(2):
            limit = (half * 128 + lane + 1) * 128
            count = jnp.zeros((256, 128), I32)
            for step in (64, 32, 16, 8, 4, 2, 1, 1):
                below = lanes(code, spot(count + (step - 1))) < limit
                count = jnp.where(below, count + step, count)
            counts.append(count)
        packed_ref[0] = (code & 127) | (counts[0] << 8) | (counts[1] << 16)


def sort_codes(pieces):
    many = len(pieces)
    return pl.pallas_call(
        sort_kernel,
        out_shape=[jax.ShapeDtypeStruct((2, 256, 128), I32)] * many,
        grid=(2,),
        in_specs=[pl.BlockSpec((1, 16, 24, 128), lambda j: (j, 0, 0, 0))] * many,
        out_specs=[pl.BlockSpec((1, 256, 128), lambda j: (j, 0, 0))] * many,
        compiler_params=pltpu.CompilerParams(vmem_limit_bytes=VMEM_LIMIT),
        cost_estimate=pl.CostEstimate(flops=many * SORT_FLOPS, bytes_accessed=many * 1024 * 1024, transcendentals=0),
    )(*pieces)


def split_kernel(where_ref, hessian_ref, right_ref):
    for j in range(8):
        for c in range(2):
            high, low = split(hessian_ref[pl.ds(c * 8 + j, 128, stride=16), :])
            cut = slice(j * 128, j * 128 + 128)
            right_ref[0, c * 128 : c * 128 + 128, cut] = high
            right_ref[0, 256 + c * 128 : 256 + c * 128 + 128, cut] = low


def split_hessian(where, rows):
    return pl.pallas_call(
        split_kernel,
        out_shape=jax.ShapeDtypeStruct((8, 512, 1024), BF16),
        grid=(8,),
        in_specs=[in_smem(), pl.BlockSpec((2048, 128), lambda q: (q, 0))],
        out_specs=pl.BlockSpec((1, 512, 1024), lambda q: (q, 0, 0)),
        compiler_params=pltpu.CompilerParams(vmem_limit_bytes=VMEM_LIMIT),
        cost_estimate=pl.CostEstimate(flops=SPLIT_FLOPS, bytes_accessed=20 * 1024 * 1024, transcendentals=0),
    )(where, rows)


def step_body(second, where_ref, packed_refs, rights, book_row_ref, refs):
    error_refs, refs = (refs[:8], refs[8:16]), refs[16:]
    if second:
        code_refs, refs = (refs[:8], refs[8:16]), refs[16:]
        (near_ref, far_ref, book_col_ref), refs = refs[:3], refs[3:]
    keep_ref, send_ref, left0_ref, left1_ref, grad_ref, sums_ref, table_ref = refs
    n = pl.program_id(0)
    row, col, place = where_ref[0], where_ref[1], where_ref[2]

    def multiply(left_ref, right_ref):
        for part in range(4):
            for m in range(2):
                rows = slice(m * 256, m * 256 + 256)
                cut = slice(part * 256, part * 256 + 256)
                more = dot_nn(left_ref[rows, 0:512], right_ref[0, :, cut]) + dot_nn(left_ref[rows, 512:768], right_ref[0, 0:256, cut])
                grad_ref[2 * part, rows, :] += more[:, 0:128]
                grad_ref[2 * part + 1, rows, :] += more[:, 128:256]

    def prepare(half, left_ref):
        b = jnp.minimum(2 * n + half, 7)
        for core in range(2):
            for kx in range(4):
                which = core * 4 + kx
                for kyh in range(2):
                    start = pl.multiple_of((col ^ (kx * 4 + kyh * 2 + core)) * 16, 16)
                    base = core * 16 + (kx * 2 + kyh) * 2
                    for c in range(2):
                        if second:
                            tables = [
                                [
                                    jnp.broadcast_to(table_ref[b, base + t : base + t + 1, (c * 2 + k) * 128 : (c * 2 + k) * 128 + 128], (8, 128))
                                    for k in range(2)
                                ]
                                for t in range(2)
                            ]
                        for parity in range(2):
                            value = error_refs[half][which][kyh, c, parity * 16 : parity * 16 + 16, :]
                            if second:
                                moves = [
                                    lookup(code_refs[half][which][kyh, parity * 16 + t * 8 : parity * 16 + t * 8 + 8, :], *tables[t])
                                    for t in range(2)
                                ]
                                value = value - jnp.concatenate(moves, axis=0)
                            high, low = split(value)
                            rows = pl.ds(parity * 256 + start, 16)
                            left_ref[rows, c * 128 : c * 128 + 128] = high
                            left_ref[rows, 256 + c * 128 : 256 + c * 128 + 128] = high
                            left_ref[rows, 512 + c * 128 : 512 + c * 128 + 128] = low

    @pl.when(n == 0)
    def _():
        left1_ref[...] = jnp.zeros((512, 768), BF16)
        grad_ref[...] = jnp.zeros((8, 512, 128), F32)
        if second:
            chosen = jnp.where((book_col_ref[...] ^ place) == iota((256, 512), 1), 1.0, 0.0).astype(BF16)
            total = jnp.zeros((256, 512), F32)
            for part, ref in ((0, near_ref), (1, far_ref)):
                high, low = split(ref[...])
                here = chosen[:, part * 256 : part * 256 + 256]
                total = total + dot_nn(here, high) + dot_nn(here, low)
            table_ref[...] = (total * LEARN_RATE).reshape(8, 32, 512)

    prepare(0, left0_ref)
    multiply(left1_ref, rights[0])

    @pl.when(n < 4)
    def _():
        prepare(1, left1_ref)
        multiply(left0_ref, rights[1])

    @pl.when(n == 4)
    def _():
        parting = part_pairs()
        running = jnp.where(spot_back(iota((256, 128), 0) & 127) <= iota((256, 128), 1), 1.0, 0.0).astype(BF16)
        lane = iota((32, 128), 1)
        for kz in range(4):
            for dyl in range(2):
                j = row ^ (dyl * 4 + kz)
                at = kz * 2 + dyl
                both = jnp.concatenate([grad_ref[j, 0:256, :], grad_ref[j, 256:512, :]], axis=1)
                high, low = split(both)
                pairs = dot_nn(high, parting) + dot_nn(low, parting)
                packed = packed_refs[kz][dyl]
                source = packed & 127
                counts = [(packed >> 8) & 255, packed >> 16]
                for c in range(2):
                    ordered = lanes(pairs[:, c * 128 : c * 128 + 128], source)
                    prefix = dot_nn(jnp.concatenate(split(ordered), axis=1), running)
                    upto = []
                    for count in counts:
                        value = jnp.where(count > 0, lanes(prefix, jnp.maximum(count - 1, 0)), 0.0)
                        upto.append(value.reshape(32, 8, 128).sum(axis=1))
                    earlier = [pltpu.roll(v, 1, 1) for v in upto]
                    low_sums = 2.0 * (upto[0] - jnp.where(lane == 0, 0.0, earlier[0]))
                    high_sums = 2.0 * (upto[1] - jnp.where(lane == 0, earlier[0], earlier[1]))
                    sums_ref[at, :, c * 256 : c * 256 + 128] = low_sums
                    sums_ref[at, :, c * 256 + 128 : c * 256 + 256] = high_sums
        chosen = jnp.where((iota((512, 256), 0) ^ place) == book_row_ref[...], 1.0, 0.0).astype(BF16)
        high, low = split(sums_ref[...].reshape(256, 512))
        total = dot_nn(chosen, high) + dot_nn(chosen, low)
        keep_ref[...] = total[0:256]
        send_ref[...] = total[256:512]


def step(second, place, packed, right, book_row, errors, codes, rest):
    def kernel(where_ref, *refs):
        step_body(second, where_ref, refs[0:4], refs[4:6], refs[6], refs[7:])

    def tile_column(half):
        return lambda n: jnp.clip(2 * n + half, 0, 7)

    right_specs, error_specs, code_specs = [], [], []
    for half in (-1, 0):
        right_specs.append(pl.BlockSpec((1, 512, 1024), lambda n, f=tile_column(half): (f(n), 0, 0)))
    for half in (0, 1):
        error_specs += [pl.BlockSpec((2, 2, 32, 128), lambda n, f=tile_column(half): (0, f(n), 0, 0))] * 8
        code_specs += [pl.BlockSpec((2, 40, 128), lambda n, f=tile_column(half): (0, 0, f(n)))] * 8
    half = jax.ShapeDtypeStruct((256, 512), F32)
    return pl.pallas_call(
        kernel,
        out_shape=[half, half],
        grid=(5,),
        in_specs=[in_smem()]
        + [whole(x) for x in packed]
        + right_specs
        + [whole(book_row)]
        + error_specs
        + (code_specs if second else [])
        + [whole(x) for x in rest],
        out_specs=[pl.BlockSpec((256, 512), lambda n: (0, 0))] * 2,
        scratch_shapes=[
            pltpu.VMEM((512, 768), BF16),
            pltpu.VMEM((512, 768), BF16),
            pltpu.VMEM((8, 512, 128), F32),
            pltpu.VMEM((8, 32, 512), F32),
            pltpu.VMEM((8, 32, 512), F32),
        ],
        compiler_params=pltpu.CompilerParams(vmem_limit_bytes=VMEM_LIMIT),
        cost_estimate=pl.CostEstimate(flops=STEP_FLOPS, bytes_accessed=16 * 1024 * 1024, transcendentals=0),
    )(place, *packed, right, right, book_row, *errors, *errors, *codes, *codes, *rest)


def update_kernel(where_ref, books_ref, near_ref, far_ref, out_ref):
    for part, ref in enumerate((near_ref, far_ref)):
        for k in range(4):
            start = pl.multiple_of((part * 256 + k * 64) ^ where_ref[2], 64)
            for c in range(2):
                moved = LEARN_RATE * ref[k * 64 : k * 64 + 64, c * 256 : c * 256 + 256]
                out_ref[pl.ds(start, 64), c, :] = books_ref[pl.ds(start, 64), c, :] - moved


def update(where, codebooks, near, far):
    return pl.pallas_call(
        update_kernel,
        out_shape=jax.ShapeDtypeStruct((512, 2, 256), F32),
        in_specs=[in_smem()] + in_vmem(3),
        out_specs=in_vmem(1)[0],
    )(where, codebooks, near, far)


def sum_all(keep, send):
    half = keep + swap(send, dcore=1)
    quarter = [half[k * 64 : k * 64 + 64] for k in range(4)]
    got = [None] + [swap(quarter[k], dx=k) for k in (1, 2, 3)]
    s = (quarter[0] + got[2]) + (got[1] + got[3])
    got = [None] + [swap(s, dyl=k & 1, dyh=k >> 1) for k in (1, 2, 3)]
    s = (s + got[2]) + (got[1] + got[3])
    got = [None] + [swap(s, dz=k) for k in (1, 2, 3)]
    s = (s + got[2]) + (got[1] + got[3])
    near = jnp.concatenate([s] + [swap(s, dx=k) for k in (1, 2, 3)])
    return near, swap(near, dcore=1)


def hold(*values):
    return lax.optimization_barrier(values)


def pair_up(own):
    return jnp.stack([own, swap(own, dyh=1)])


def over_x(pair):
    return [pair] + [swap(pair, dx=k) for k in (1, 2, 3)]


def both_cores(near):
    return list(near) + [swap(v, dcore=1) for v in near]


def per_device(hessian, weights, codes, tile_map, codebooks):
    row, col = lax.axis_index("row").astype(I32), lax.axis_index("col").astype(I32)
    where = jnp.stack([row, col, (col & 1) * 256 + (col >> 2) * 64])
    pieces, own = make_pieces(codes, tile_map)
    pieces = lax.all_to_all(pieces, "col", 0, 0, tiled=True)
    error_pair = pair_up(first(weights, own, tile_map, codebooks))
    pieces, error_pair, own = hold(pieces, error_pair, own)

    errors = over_x(error_pair)
    pieces = jnp.stack([pieces, swap(pieces, dyl=1)])
    pieces, later = hold(pieces, where)
    code_pair = pair_up(own)
    right = split_hessian(later, hessian.reshape(16384, 128))
    packed = sort_codes([pieces])
    held = hold(right, code_pair, *packed, *[swap(pieces, dz=k) for k in (1, 2, 3)])
    right, code_pair, packed, others = held[0], held[1], list(held[2:3]), list(held[3:])
    packed += sort_codes(others)
    book_row = jnp.concatenate([v[:, :, 16, 0:2] for v in [pieces] + others]).reshape(1, 256)
    held = hold(book_row, *packed, *errors, *over_x(code_pair))
    book_row, packed, errors, around = held[0], held[1:5], held[5:9], held[9:]
    errors = both_cores(errors)
    keep, send = step(False, where, packed, right, book_row, errors, [], [])
    around = both_cores(around)
    book_col = jnp.concatenate([v[:, 32:34, 0:8] for v in around]).reshape(32, 8).T.reshape(256, 1)
    near, far = sum_all(keep, send)
    keep, send = step(True, where, packed, right, book_row, errors, around, [near, far, book_col])
    codebooks = update(where, codebooks, near, far)
    return update(where, codebooks, *sum_all(keep, send))


def solution(mesh):
    placed = (P("row", None, "col", None), P("col", "row"), P("col", "row"), P("col", "row"), P())
    return jax.shard_map(per_device, mesh=mesh, in_specs=placed, out_specs=P(), check_vma=False)
```

```python
import jax
import jax.numpy as jnp
from jax import lax
from jax.experimental import pallas as pl
from jax.experimental.pallas import tpu as pltpu
from jax.sharding import PartitionSpec as P

F32 = jnp.float32
BF16 = jnp.bfloat16
I32 = jnp.int32
LEARN_RATE = 0.01
BOTH = ("row", "col")
VMEM_LIMIT = 56 * 1024 * 1024
STEP_FLOPS = 18 * 10**9
SORT_FLOPS = 5 * 10**9
SPLIT_FLOPS = 9 * 10**9


def partners(dx, dyh, dcore, dyl, dz):
    flip_col = dx * 4 + dyh * 2 + dcore
    flip_row = dyl * 4 + dz
    return [(i, i ^ (flip_row * 16 + flip_col)) for i in range(128)]


def swap(v, dx=0, dyh=0, dcore=0, dyl=0, dz=0):
    return lax.ppermute(v, BOTH, partners(dx, dyh, dcore, dyl, dz))


def lanes(x, index):
    return jnp.take_along_axis(x, index, axis=1, mode="promise_in_bounds")


def iota(shape, dim):
    return lax.broadcasted_iota(I32, shape, dim)


def split(x):
    high = x.astype(BF16)
    low = (x - high.astype(F32)).astype(BF16)
    return high, low


def dot_nt(a, b):
    return lax.dot_general(a, b, (((1,), (1,)), ((), ())), preferred_element_type=F32)


def dot_nn(a, b):
    return lax.dot_general(a, b, (((1,), (0,)), ((), ())), preferred_element_type=F32)


def whole(x):
    return pl.BlockSpec(x.shape, lambda *_: (0,) * x.ndim)


def in_vmem(n):
    return [pl.BlockSpec(memory_space=pltpu.VMEM)] * n


def in_smem():
    return pl.BlockSpec(memory_space=pltpu.SMEM)


def lookup(code, low_table, high_table):
    low = code & 127
    return jnp.where(code >= 128, lanes(high_table, low), lanes(low_table, low))


def part_pairs():
    lane = iota((256, 256), 1)
    return jnp.where(iota((256, 256), 0) == 2 * (lane & 127) + (lane >> 7), 1.0, 0.0).astype(BF16)


def tile_rows(start, tile, parity):
    return pl.ds(start + tile * 16 + parity, 8, stride=2)


def pieces_kernel(tile_ref, codes_ref, piece_ref, own_ref, held_ref):
    lane = iota((8, 128), 1)
    left = lane < 64
    for q in range(8):
        cut = slice(q * 128, q * 128 + 128)
        held_ref[q * 32 : q * 32 + 32, :] = codes_ref[:, cut]
        for t in range(2):
            even = held_ref[tile_rows(q * 32, t, 0), :]
            odd = held_ref[tile_rows(q * 32, t, 1), :]
            own_ref[t * 8 : t * 8 + 8, cut] = even
            own_ref[16 + t * 8 : 24 + t * 8, cut] = odd
            pair = [
                jnp.where(left, even, pltpu.roll(odd, 64, 1)),
                jnp.where(left, pltpu.roll(even, 64, 1), odd),
            ]
            for h in range(2):
                piece_ref[2 * q + h, t * 8 : t * 8 + 8, :] = pair[h]
        books = jnp.where((lane & 1) == 0, tile_ref[0, q], tile_ref[1, q])
        for h in range(2):
            piece_ref[2 * q + h, 16:24, :] = books


def make_pieces(codes, tile_map):
    return pl.pallas_call(
        pieces_kernel,
        out_shape=[jax.ShapeDtypeStruct((16, 24, 128), I32), jax.ShapeDtypeStruct((32, 1024), I32)],
        in_specs=[in_smem()] + in_vmem(1),
        out_specs=in_vmem(2),
        scratch_shapes=[pltpu.VMEM((256, 128), I32)],
    )(tile_map, codes)


def first_kernel(tile_ref, weights_ref, own_ref, books_ref, out_ref, weight_ref):
    parting = part_pairs()
    for q in range(8):
        parted = dot_nn(weights_ref[:, q * 256 : q * 256 + 256], parting)
        weight_ref[q * 64 : q * 64 + 32, :] = parted[:, 0:128]
        weight_ref[q * 64 + 32 : q * 64 + 64, :] = parted[:, 128:256]
    for q in range(8):
        for t in range(2):
            book = books_ref[tile_ref[t, q]]
            for c in range(2):
                tables = [jnp.broadcast_to(book[c : c + 1, k * 128 : k * 128 + 128], (8, 128)) for k in range(2)]
                for parity in range(2):
                    row = parity * 16 + t * 8
                    code = own_ref[row : row + 8, q * 128 : q * 128 + 128]
                    weight = weight_ref[tile_rows((q * 2 + c) * 32, t, parity), :]
                    out_ref[q, c * 32 + row : c * 32 + row + 8, :] = lookup(code, *tables) - weight
        out_ref[q, 64:96, :] = own_ref[:, q * 128 : q * 128 + 128].astype(F32)
        out_ref[q, 96:104, :] = jnp.where(iota((8, 128), 0) == 0, tile_ref[0, q], tile_ref[1, q]).astype(F32)


def first(weights, own, tile_map, codebooks):
    return pl.pallas_call(
        first_kernel,
        out_shape=jax.ShapeDtypeStruct((8, 104, 128), F32),
        in_specs=[in_smem()] + in_vmem(3),
        out_specs=in_vmem(1)[0],
        scratch_shapes=[pltpu.VMEM((512, 128), F32)],
    )(tile_map, weights, own, codebooks)


def spot(position):
    return ((position & 15) << 3) | (position >> 4)


def spot_back(lane):
    return ((lane & 7) << 4) | (lane >> 3)


def sort_block(keys):
    rows = [keys[v * 8 : v * 8 + 8, :] for v in range(16)]
    sub = iota((8, 128), 0)
    k = 2
    while k <= 128:
        j = k // 2
        while j >= 1:
            if j < 16:
                for v in range(16):
                    if v & j:
                        continue
                    a, b = rows[v], rows[v | j]
                    small, large = jnp.minimum(a, b), jnp.maximum(a, b)
                    if k < 16:
                        rising = (v & k) == 0
                        rows[v], rows[v | j] = (small, large) if rising else (large, small)
                    elif k == 128:
                        rows[v], rows[v | j] = small, large
                    else:
                        up = (sub & (k >> 4)) == 0
                        rows[v], rows[v | j] = jnp.where(up, small, large), jnp.where(up, large, small)
            else:
                step = j >> 4
                lower = (sub & step) == 0
                up = lower if k == 128 else ((sub & (k >> 4)) == 0) == lower
                for v in range(16):
                    other = jnp.where(lower, pltpu.roll(rows[v], 8 - step, 0), pltpu.roll(rows[v], step, 0))
                    rows[v] = jnp.where(up, jnp.minimum(rows[v], other), jnp.maximum(rows[v], other))
            j //= 2
        k *= 2
    return jnp.concatenate(rows, axis=0)


def sort_body(first_kz, *refs):
    lane = iota((256, 128), 1)
    spot32 = iota((8, 128), 1) >> 1
    for n, (piece_ref, packed_ref) in enumerate(zip(refs[: len(refs) // 2], refs[len(refs) // 2 :])):
        base = ((first_kz + n) % 2) * 32 + pl.program_id(0) * 16
        books = jnp.zeros((8, 128), I32)
        for origin in range(16):
            books = jnp.where(spot32 == base + origin, piece_ref[0, origin, 16:24, :], books)
        packed_ref[0, 256:264, :] = books
        key = (piece_ref[0, :, 0:16, :].reshape(256, 128) * 128 + lane).astype(F32)
        halves = [sort_block(key[h * 128 : h * 128 + 128, :].T).T for h in range(2)]
        code = jnp.concatenate(halves, axis=0).astype(I32)
        counts = []
        for half in range(2):
            limit = (half * 128 + lane + 1) * 128
            count = jnp.zeros((256, 128), I32)
            for step in (64, 32, 16, 8, 4, 2, 1, 1):
                below = lanes(code, spot(count + (step - 1))) < limit
                count = jnp.where(below, count + step, count)
            counts.append(count)
        packed_ref[0, 0:256, :] = (code & 127) | (counts[0] << 8) | (counts[1] << 16)


def sort_codes(pieces, first_kz):
    many = len(pieces)

    def sort_kernel(*refs):
        sort_body(first_kz, *refs)

    return pl.pallas_call(
        sort_kernel,
        out_shape=[jax.ShapeDtypeStruct((2, 264, 128), I32)] * many,
        grid=(2,),
        in_specs=[pl.BlockSpec((1, 16, 24, 128), lambda j: (j, 0, 0, 0))] * many,
        out_specs=[pl.BlockSpec((1, 264, 128), lambda j: (j, 0, 0))] * many,
        compiler_params=pltpu.CompilerParams(vmem_limit_bytes=VMEM_LIMIT),
        cost_estimate=pl.CostEstimate(flops=many * SORT_FLOPS, bytes_accessed=many * 1024 * 1024, transcendentals=0),
    )(*pieces)


def split_kernel(where_ref, hessian_ref, right_ref):
    for j in range(8):
        for c in range(2):
            high, low = split(hessian_ref[pl.ds(c * 8 + j, 128, stride=16), :])
            cut = slice(j * 128, j * 128 + 128)
            right_ref[0, c * 128 : c * 128 + 128, cut] = high
            right_ref[0, 256 + c * 128 : 256 + c * 128 + 128, cut] = low


def split_hessian(where, rows):
    return pl.pallas_call(
        split_kernel,
        out_shape=jax.ShapeDtypeStruct((8, 512, 1024), BF16),
        grid=(8,),
        in_specs=[in_smem(), pl.BlockSpec((2048, 128), lambda q: (q, 0))],
        out_specs=pl.BlockSpec((1, 512, 1024), lambda q: (q, 0, 0)),
        compiler_params=pltpu.CompilerParams(vmem_limit_bytes=VMEM_LIMIT),
        cost_estimate=pl.CostEstimate(flops=SPLIT_FLOPS, bytes_accessed=20 * 1024 * 1024, transcendentals=0),
    )(where, rows)


def step_body(second, where_ref, packed_refs, rights, refs):
    error_refs, refs = (refs[:8], refs[8:16]), refs[16:]
    if second:
        (near_ref, far_ref, book_col_ref), refs = refs[:3], refs[3:]
    keep_ref, send_ref, left0_ref, left1_ref, grad_ref, sums_ref, table_ref = refs
    n = pl.program_id(0)
    row, col, place = where_ref[0], where_ref[1], where_ref[2]

    def multiply(left_ref, right_ref):
        for part in range(4):
            for m in range(2):
                rows = slice(m * 256, m * 256 + 256)
                cut = slice(part * 256, part * 256 + 256)
                more = dot_nn(left_ref[rows, 0:512], right_ref[0, :, cut]) + dot_nn(left_ref[rows, 512:768], right_ref[0, 0:256, cut])
                grad_ref[2 * part, rows, :] += more[:, 0:128]
                grad_ref[2 * part + 1, rows, :] += more[:, 128:256]

    def prepare(half, left_ref):
        b = jnp.minimum(2 * n + half, 7)
        for core in range(2):
            for kx in range(4):
                which = core * 4 + kx
                for kyh in range(2):
                    start = pl.multiple_of((col ^ (kx * 4 + kyh * 2 + core)) * 16, 16)
                    base = core * 16 + (kx * 2 + kyh) * 2
                    for c in range(2):
                        if second:
                            tables = [
                                [
                                    jnp.broadcast_to(table_ref[b, base + t : base + t + 1, (c * 2 + k) * 128 : (c * 2 + k) * 128 + 128], (8, 128))
                                    for k in range(2)
                                ]
                                for t in range(2)
                            ]
                        for parity in range(2):
                            row = c * 32 + parity * 16
                            value = error_refs[half][which][kyh, 0, row : row + 16, :]
                            if second:
                                row = 64 + parity * 16
                                code = error_refs[half][which][kyh, 0, row : row + 16, :].astype(I32)
                                moves = [lookup(code[t * 8 : t * 8 + 8], *tables[t]) for t in range(2)]
                                value = value - jnp.concatenate(moves, axis=0)
                            high, low = split(value)
                            rows = pl.ds(parity * 256 + start, 16)
                            left_ref[rows, c * 128 : c * 128 + 128] = high
                            left_ref[rows, 256 + c * 128 : 256 + c * 128 + 128] = high
                            left_ref[rows, 512 + c * 128 : 512 + c * 128 + 128] = low

    @pl.when(n == 0)
    def _():
        left1_ref[...] = jnp.zeros((512, 768), BF16)
        grad_ref[...] = jnp.zeros((8, 512, 128), F32)
        if second:
            chosen = jnp.where((book_col_ref[...] ^ place) == iota((256, 512), 1), 1.0, 0.0).astype(BF16)
            total = jnp.zeros((256, 512), F32)
            for part, ref in ((0, near_ref), (1, far_ref)):
                high, low = split(ref[...])
                here = chosen[:, part * 256 : part * 256 + 256]
                total = total + dot_nn(here, high) + dot_nn(here, low)
            table_ref[...] = (total * LEARN_RATE).reshape(8, 32, 512)

    prepare(0, left0_ref)
    multiply(left1_ref, rights[0])

    @pl.when(n < 4)
    def _():
        prepare(1, left1_ref)
        multiply(left0_ref, rights[1])

    @pl.when(n == 4)
    def _():
        parting = part_pairs()
        running = jnp.where(spot_back(iota((256, 128), 0) & 127) <= iota((256, 128), 1), 1.0, 0.0).astype(BF16)
        lane = iota((32, 128), 1)
        for kz in range(4):
            for dyl in range(2):
                j = row ^ (dyl * 4 + kz)
                at = kz * 2 + dyl
                both = jnp.concatenate([grad_ref[j, 0:256, :], grad_ref[j, 256:512, :]], axis=1)
                high, low = split(both)
                pairs = dot_nn(high, parting) + dot_nn(low, parting)
                packed = packed_refs[kz][dyl, 0:256, :]
                source = packed & 127
                counts = [(packed >> 8) & 255, packed >> 16]
                for c in range(2):
                    ordered = lanes(pairs[:, c * 128 : c * 128 + 128], source)
                    prefix = dot_nn(jnp.concatenate(split(ordered), axis=1), running)
                    upto = []
                    for count in counts:
                        value = jnp.where(count > 0, lanes(prefix, jnp.maximum(count - 1, 0)), 0.0)
                        upto.append(value.reshape(32, 8, 128).sum(axis=1))
                    earlier = [pltpu.roll(v, 1, 1) for v in upto]
                    low_sums = 2.0 * (upto[0] - jnp.where(lane == 0, 0.0, earlier[0]))
                    high_sums = 2.0 * (upto[1] - jnp.where(lane == 0, earlier[0], earlier[1]))
                    sums_ref[at, :, c * 256 : c * 256 + 128] = low_sums
                    sums_ref[at, :, c * 256 + 128 : c * 256 + 256] = high_sums
        books = [packed_refs[kz][0, 256:257, :] + packed_refs[kz][1, 256:257, :] for kz in range(4)]
        books = jnp.concatenate([books[0] + books[1], books[2] + books[3]], axis=1)
        chosen = jnp.where((iota((512, 256), 0) ^ place) == books, 1.0, 0.0).astype(BF16)
        high, low = split(sums_ref[...].reshape(256, 512))
        total = dot_nn(chosen, high) + dot_nn(chosen, low)
        keep_ref[...] = total[0:256]
        send_ref[...] = total[256:512]


def step(second, place, packed, right, errors, rest):
    def kernel(where_ref, *refs):
        step_body(second, where_ref, refs[0:4], refs[4:6], refs[6:])

    def tile_column(half):
        return lambda n: jnp.clip(2 * n + half, 0, 7)

    right_specs, error_specs = [], []
    height = 104 if second else 64
    for half in (-1, 0):
        right_specs.append(pl.BlockSpec((1, 512, 1024), lambda n, f=tile_column(half): (f(n), 0, 0)))
    for half in (0, 1):
        error_specs += [pl.BlockSpec((2, 1, height, 128), lambda n, f=tile_column(half): (0, f(n), 0, 0))] * 8
    half = jax.ShapeDtypeStruct((256, 512), F32)
    return pl.pallas_call(
        kernel,
        out_shape=[half, half],
        grid=(5,),
        in_specs=[in_smem()]
        + [whole(x) for x in packed]
        + right_specs
        + error_specs
        + [whole(x) for x in rest],
        out_specs=[pl.BlockSpec((256, 512), lambda n: (0, 0))] * 2,
        scratch_shapes=[
            pltpu.VMEM((512, 768), BF16),
            pltpu.VMEM((512, 768), BF16),
            pltpu.VMEM((8, 512, 128), F32),
            pltpu.VMEM((8, 32, 512), F32),
            pltpu.VMEM((8, 32, 512), F32),
        ],
        compiler_params=pltpu.CompilerParams(vmem_limit_bytes=VMEM_LIMIT),
        cost_estimate=pl.CostEstimate(flops=STEP_FLOPS, bytes_accessed=16 * 1024 * 1024, transcendentals=0),
    )(place, *packed, right, right, *errors, *errors, *rest)


def update_kernel(where_ref, books_ref, near_ref, far_ref, out_ref):
    for part, ref in enumerate((near_ref, far_ref)):
        for k in range(4):
            start = pl.multiple_of((part * 256 + k * 64) ^ where_ref[2], 64)
            for c in range(2):
                moved = LEARN_RATE * ref[k * 64 : k * 64 + 64, c * 256 : c * 256 + 256]
                out_ref[pl.ds(start, 64), c, :] = books_ref[pl.ds(start, 64), c, :] - moved


def update(where, codebooks, near, far):
    return pl.pallas_call(
        update_kernel,
        out_shape=jax.ShapeDtypeStruct((512, 2, 256), F32),
        in_specs=[in_smem()] + in_vmem(3),
        out_specs=in_vmem(1)[0],
    )(where, codebooks, near, far)


def sum_all(keep, send, beside):
    half = keep + swap(send, dcore=1)
    quarter = [half[k * 64 : k * 64 + 64] for k in range(4)]
    got = [None] + [swap(quarter[k], dx=k) for k in (1, 2, 3)]
    s = (quarter[0] + got[2]) + (got[1] + got[3])
    s, beside = hold(s, beside)
    got = [None] + [swap(s, dyl=k & 1, dyh=k >> 1) for k in (1, 2, 3)]
    s = (s + got[2]) + (got[1] + got[3])
    got = [None] + [swap(s, dz=k) for k in (1, 2, 3)]
    s = (s + got[2]) + (got[1] + got[3])
    near = jnp.concatenate([s] + [swap(s, dx=k) for k in (1, 2, 3)])
    return near, swap(near, dcore=1), beside


def hold(*values):
    return lax.optimization_barrier(values)


def pair_up(own):
    return jnp.stack([own, swap(own, dyh=1)])


def over_x(pair):
    return [pair] + [swap(pair, dx=k) for k in (1, 2, 3)]


def both_cores(near):
    return list(near) + [swap(v, dcore=1) for v in near]


def per_device(hessian, weights, codes, tile_map, codebooks):
    row, col = lax.axis_index("row").astype(I32), lax.axis_index("col").astype(I32)
    where = jnp.stack([row, col, (col & 1) * 256 + (col >> 2) * 64])
    pieces, own = make_pieces(codes, tile_map)
    pieces = lax.all_to_all(pieces, "col", 0, 0, tiled=True)
    pair = pair_up(first(weights, own, tile_map, codebooks))
    pieces, pair = hold(pieces, pair)

    around = over_x(pair)
    pieces = jnp.stack([pieces, swap(pieces, dyl=1)])
    pieces, later = hold(pieces, where)
    right = split_hessian(later, hessian.reshape(16384, 128))
    packed = sort_codes([pieces], 0)
    right, packed, one, three = hold(right, packed, *[swap(pieces, dz=k) for k in (1, 3)])
    pieces, one = hold(pieces, one)
    two = swap(pieces, dz=2)
    packed_one, packed_three = sort_codes([one], 1), sort_codes([three], 3)
    packed_one, packed_three, *around = hold(packed_one, packed_three, *around)
    around = both_cores(around)
    packed = [*packed, *packed_one, *sort_codes([two], 2), *packed_three]
    keep, send = step(False, where, packed, right, around, [])
    book_col = jnp.concatenate([v[:, :, 96:98, 0] for v in around])
    book_col = book_col.transpose(1, 0, 2).reshape(256, 1).astype(I32)
    near, far, book_col = sum_all(keep, send, book_col)
    keep, send = step(True, where, packed, right, around, [near, far, book_col])
    near, far, codebooks = sum_all(keep, send, update(where, codebooks, near, far))
    return update(where, codebooks, near, far)


def solution(mesh):
    placed = (P("row", None, "col", None), P("col", "row"), P("col", "row"), P("col", "row"), P())
    return jax.shard_map(per_device, mesh=mesh, in_specs=placed, out_specs=P(), check_vma=False)
```

```python
import jax
import jax.numpy as jnp
from jax import lax
from jax.experimental import pallas as pl
from jax.experimental.pallas import tpu as pltpu
from jax.sharding import PartitionSpec as P

F32 = jnp.float32
BF16 = jnp.bfloat16
I32 = jnp.int32
LEARN_RATE = 0.01
BOTH = ("row", "col")
VMEM_LIMIT = 56 * 1024 * 1024
STEP_FLOPS = 18 * 10**9
SORT_FLOPS = 5 * 10**9
SPLIT_FLOPS = 9 * 10**9


def partners(dx, dyh, dcore, dyl, dz):
    flip_col = dx * 4 + dyh * 2 + dcore
    flip_row = dyl * 4 + dz
    return [(i, i ^ (flip_row * 16 + flip_col)) for i in range(128)]


def swap(v, dx=0, dyh=0, dcore=0, dyl=0, dz=0):
    return lax.ppermute(v, BOTH, partners(dx, dyh, dcore, dyl, dz))


def lanes(x, index):
    return jnp.take_along_axis(x, index, axis=1, mode="promise_in_bounds")


def iota(shape, dim):
    return lax.broadcasted_iota(I32, shape, dim)


def split(x):
    high = x.astype(BF16)
    low = (x - high.astype(F32)).astype(BF16)
    return high, low


def dot_nt(a, b):
    return lax.dot_general(a, b, (((1,), (1,)), ((), ())), preferred_element_type=F32)


def dot_nn(a, b):
    return lax.dot_general(a, b, (((1,), (0,)), ((), ())), preferred_element_type=F32)


def whole(x):
    return pl.BlockSpec(x.shape, lambda *_: (0,) * x.ndim)


def in_vmem(n):
    return [pl.BlockSpec(memory_space=pltpu.VMEM)] * n


def in_smem():
    return pl.BlockSpec(memory_space=pltpu.SMEM)


def lookup(code, low_table, high_table):
    low = code & 127
    return jnp.where(code >= 128, lanes(high_table, low), lanes(low_table, low))


def part_pairs():
    lane = iota((256, 256), 1)
    return jnp.where(iota((256, 256), 0) == 2 * (lane & 127) + (lane >> 7), 1.0, 0.0).astype(BF16)


def tile_rows(start, tile, parity):
    return pl.ds(start + tile * 16 + parity, 8, stride=2)


def pieces_kernel(tile_ref, codes_ref, piece_ref, own_ref, held_ref):
    lane = iota((8, 128), 1)
    left = lane < 64
    for q in range(8):
        cut = slice(q * 128, q * 128 + 128)
        held_ref[q * 32 : q * 32 + 32, :] = codes_ref[:, cut]
        for t in range(2):
            even = held_ref[tile_rows(q * 32, t, 0), :]
            odd = held_ref[tile_rows(q * 32, t, 1), :]
            own_ref[t * 8 : t * 8 + 8, cut] = even
            own_ref[16 + t * 8 : 24 + t * 8, cut] = odd
            pair = [
                jnp.where(left, even, pltpu.roll(odd, 64, 1)),
                jnp.where(left, pltpu.roll(even, 64, 1), odd),
            ]
            for h in range(2):
                piece_ref[2 * q + h, t * 8 : t * 8 + 8, :] = pair[h]
        books = jnp.where((lane & 1) == 0, tile_ref[0, q], tile_ref[1, q])
        for h in range(2):
            piece_ref[2 * q + h, 16:24, :] = books


def make_pieces(codes, tile_map):
    return pl.pallas_call(
        pieces_kernel,
        out_shape=[jax.ShapeDtypeStruct((16, 24, 128), I32), jax.ShapeDtypeStruct((32, 1024), I32)],
        in_specs=[in_smem()] + in_vmem(1),
        out_specs=in_vmem(2),
        scratch_shapes=[pltpu.VMEM((256, 128), I32)],
    )(tile_map, codes)


def first_kernel(tile_ref, weights_ref, own_ref, books_ref, out_ref, weight_ref):
    parting = part_pairs()
    for q in range(8):
        parted = dot_nn(weights_ref[:, q * 256 : q * 256 + 256], parting)
        weight_ref[q * 64 : q * 64 + 32, :] = parted[:, 0:128]
        weight_ref[q * 64 + 32 : q * 64 + 64, :] = parted[:, 128:256]
    for q in range(8):
        for t in range(2):
            book = books_ref[tile_ref[t, q]]
            for c in range(2):
                tables = [jnp.broadcast_to(book[c : c + 1, k * 128 : k * 128 + 128], (8, 128)) for k in range(2)]
                for parity in range(2):
                    row = parity * 16 + t * 8
                    code = own_ref[row : row + 8, q * 128 : q * 128 + 128]
                    weight = weight_ref[tile_rows((q * 2 + c) * 32, t, parity), :]
                    out_ref[q, c * 32 + row : c * 32 + row + 8, :] = lookup(code, *tables) - weight
        out_ref[q, 64:96, :] = own_ref[:, q * 128 : q * 128 + 128].astype(F32)
        out_ref[q, 96:104, :] = jnp.where(iota((8, 128), 0) == 0, tile_ref[0, q], tile_ref[1, q]).astype(F32)


def first(weights, own, tile_map, codebooks):
    return pl.pallas_call(
        first_kernel,
        out_shape=jax.ShapeDtypeStruct((8, 104, 128), F32),
        in_specs=[in_smem()] + in_vmem(3),
        out_specs=in_vmem(1)[0],
        scratch_shapes=[pltpu.VMEM((512, 128), F32)],
    )(tile_map, weights, own, codebooks)


def spot(position):
    return ((position & 15) << 3) | (position >> 4)


def spot_back(lane):
    return ((lane & 7) << 4) | (lane >> 3)


def sort_block(keys):
    rows = [keys[v * 8 : v * 8 + 8, :] for v in range(16)]
    sub = iota((8, 128), 0)
    k = 2
    while k <= 128:
        j = k // 2
        while j >= 1:
            if j < 16:
                for v in range(16):
                    if v & j:
                        continue
                    a, b = rows[v], rows[v | j]
                    small, large = jnp.minimum(a, b), jnp.maximum(a, b)
                    if k < 16:
                        rising = (v & k) == 0
                        rows[v], rows[v | j] = (small, large) if rising else (large, small)
                    elif k == 128:
                        rows[v], rows[v | j] = small, large
                    else:
                        up = (sub & (k >> 4)) == 0
                        rows[v], rows[v | j] = jnp.where(up, small, large), jnp.where(up, large, small)
            else:
                step = j >> 4
                lower = (sub & step) == 0
                up = lower if k == 128 else ((sub & (k >> 4)) == 0) == lower
                for v in range(16):
                    other = jnp.where(lower, pltpu.roll(rows[v], 8 - step, 0), pltpu.roll(rows[v], step, 0))
                    rows[v] = jnp.where(up, jnp.minimum(rows[v], other), jnp.maximum(rows[v], other))
            j //= 2
        k *= 2
    return jnp.concatenate(rows, axis=0)


def sort_body(first_kz, *refs):
    lane = iota((256, 128), 1)
    spot32 = iota((8, 128), 1) >> 1
    for n, (piece_ref, packed_ref) in enumerate(zip(refs[: len(refs) // 2], refs[len(refs) // 2 :])):
        base = ((first_kz + n) % 2) * 32 + pl.program_id(0) * 16
        books = jnp.zeros((8, 128), I32)
        for origin in range(16):
            books = jnp.where(spot32 == base + origin, piece_ref[0, origin, 16:24, :], books)
        packed_ref[0, 256:264, :] = books
        key = (piece_ref[0, :, 0:16, :].reshape(256, 128) * 128 + lane).astype(F32)
        halves = [sort_block(key[h * 128 : h * 128 + 128, :].T).T for h in range(2)]
        code = jnp.concatenate(halves, axis=0).astype(I32)
        counts = []
        for half in range(2):
            limit = (half * 128 + lane + 1) * 128
            count = jnp.zeros((256, 128), I32)
            for step in (64, 32, 16, 8, 4, 2, 1, 1):
                below = lanes(code, spot(count + (step - 1))) < limit
                count = jnp.where(below, count + step, count)
            counts.append(count)
        packed_ref[0, 0:256, :] = (code & 127) | (counts[0] << 8) | (counts[1] << 16)


def sort_codes(pieces, first_kz):
    many = len(pieces)

    def sort_kernel(*refs):
        sort_body(first_kz, *refs)

    return pl.pallas_call(
        sort_kernel,
        out_shape=[jax.ShapeDtypeStruct((2, 264, 128), I32)] * many,
        grid=(2,),
        in_specs=[pl.BlockSpec((1, 16, 24, 128), lambda j: (j, 0, 0, 0))] * many,
        out_specs=[pl.BlockSpec((1, 264, 128), lambda j: (j, 0, 0))] * many,
        compiler_params=pltpu.CompilerParams(vmem_limit_bytes=VMEM_LIMIT),
        cost_estimate=pl.CostEstimate(flops=many * SORT_FLOPS, bytes_accessed=many * 1024 * 1024, transcendentals=0),
    )(*pieces)


def split_kernel(where_ref, hessian_ref, right_ref):
    for j in range(8):
        for c in range(2):
            high, low = split(hessian_ref[pl.ds(c * 8 + j, 128, stride=16), :])
            cut = slice(j * 128, j * 128 + 128)
            right_ref[0, c * 128 : c * 128 + 128, cut] = high
            right_ref[0, 256 + c * 128 : 256 + c * 128 + 128, cut] = low


def split_hessian(where, rows):
    return pl.pallas_call(
        split_kernel,
        out_shape=jax.ShapeDtypeStruct((8, 512, 1024), BF16),
        grid=(8,),
        in_specs=[in_smem(), pl.BlockSpec((2048, 128), lambda q: (q, 0))],
        out_specs=pl.BlockSpec((1, 512, 1024), lambda q: (q, 0, 0)),
        compiler_params=pltpu.CompilerParams(vmem_limit_bytes=VMEM_LIMIT),
        cost_estimate=pl.CostEstimate(flops=SPLIT_FLOPS, bytes_accessed=20 * 1024 * 1024, transcendentals=0),
    )(where, rows)


def step_body(second, where_ref, packed_refs, rights, refs):
    error_refs, refs = (refs[:8], refs[8:16]), refs[16:]
    if second:
        (near_ref, far_ref), refs = refs[:2], refs[2:]
    keep_ref, send_ref, left0_ref, left1_ref, grad_ref, sums_ref, high_ref, low_ref, ids_ref, table_ref = refs
    n = pl.program_id(0)
    row, col, place = where_ref[0], where_ref[1], where_ref[2]

    def multiply(left_ref, right_ref):
        for part in range(4):
            for m in range(2):
                rows = slice(m * 256, m * 256 + 256)
                cut = slice(part * 256, part * 256 + 256)
                more = dot_nn(left_ref[rows, 0:512], right_ref[0, :, cut]) + dot_nn(left_ref[rows, 512:768], right_ref[0, 0:256, cut])
                grad_ref[2 * part, rows, :] += more[:, 0:128]
                grad_ref[2 * part + 1, rows, :] += more[:, 128:256]

    def prepare(half, left_ref):
        if second:
            for which in range(8):
                for kyh in range(2):
                    at = which * 4 + kyh * 2
                    ids_ref[half, at : at + 2, :] = error_refs[half][which][kyh, 0, 96:98, :]
            ids = ids_ref[half].astype(I32) ^ place
            lane = iota((32, 128), 1)
            chosen = [jnp.where(ids == lane + k * 128, 1.0, 0.0) for k in range(4)]
            chosen = jnp.concatenate(chosen, axis=1).astype(BF16)
            table_ref[half] = LEARN_RATE * (dot_nn(chosen, high_ref[...]) + dot_nn(chosen, low_ref[...]))
        for core in range(2):
            for kx in range(4):
                which = core * 4 + kx
                for kyh in range(2):
                    start = pl.multiple_of((col ^ (kx * 4 + kyh * 2 + core)) * 16, 16)
                    base = which * 4 + kyh * 2
                    for c in range(2):
                        if second:
                            tables = [
                                [
                                    jnp.broadcast_to(table_ref[half, base + t : base + t + 1, (c * 2 + k) * 128 : (c * 2 + k) * 128 + 128], (8, 128))
                                    for k in range(2)
                                ]
                                for t in range(2)
                            ]
                        for parity in range(2):
                            row = c * 32 + parity * 16
                            value = error_refs[half][which][kyh, 0, row : row + 16, :]
                            if second:
                                row = 64 + parity * 16
                                code = error_refs[half][which][kyh, 0, row : row + 16, :].astype(I32)
                                moves = [lookup(code[t * 8 : t * 8 + 8], *tables[t]) for t in range(2)]
                                value = value - jnp.concatenate(moves, axis=0)
                            high, low = split(value)
                            rows = pl.ds(parity * 256 + start, 16)
                            left_ref[rows, c * 128 : c * 128 + 128] = high
                            left_ref[rows, 256 + c * 128 : 256 + c * 128 + 128] = high
                            left_ref[rows, 512 + c * 128 : 512 + c * 128 + 128] = low

    @pl.when(n == 0)
    def _():
        left1_ref[...] = jnp.zeros((512, 768), BF16)
        grad_ref[...] = jnp.zeros((8, 512, 128), F32)
        if second:
            high_ref[0:256, :], low_ref[0:256, :] = split(near_ref[...])
            high_ref[256:512, :], low_ref[256:512, :] = split(far_ref[...])

    prepare(0, left0_ref)
    multiply(left1_ref, rights[0])

    @pl.when(n < 4)
    def _():
        prepare(1, left1_ref)
        multiply(left0_ref, rights[1])

    @pl.when(n == 4)
    def _():
        parting = part_pairs()
        running = jnp.where(spot_back(iota((256, 128), 0) & 127) <= iota((256, 128), 1), 1.0, 0.0).astype(BF16)
        lane = iota((32, 128), 1)
        for kz in range(4):

            def sum_codes(dyl, carry, kz=kz):
                j = row ^ (dyl * 4 + kz)
                at = kz * 2 + dyl
                both = jnp.concatenate([grad_ref[j, 0:256, :], grad_ref[j, 256:512, :]], axis=1)
                high, low = split(both)
                pairs = dot_nn(high, parting) + dot_nn(low, parting)
                packed = packed_refs[kz][dyl, 0:256, :]
                source = packed & 127
                counts = [(packed >> 8) & 255, packed >> 16]
                for c in range(2):
                    ordered = lanes(pairs[:, c * 128 : c * 128 + 128], source)
                    prefix = dot_nn(jnp.concatenate(split(ordered), axis=1), running)
                    upto = []
                    for count in counts:
                        value = jnp.where(count > 0, lanes(prefix, jnp.maximum(count - 1, 0)), 0.0)
                        upto.append(value.reshape(32, 8, 128).sum(axis=1))
                    earlier = [pltpu.roll(v, 1, 1) for v in upto]
                    low_sums = 2.0 * (upto[0] - jnp.where(lane == 0, 0.0, earlier[0]))
                    high_sums = 2.0 * (upto[1] - jnp.where(lane == 0, earlier[0], earlier[1]))
                    sums_ref[at, :, c * 256 : c * 256 + 128] = low_sums
                    sums_ref[at, :, c * 256 + 128 : c * 256 + 256] = high_sums
                return carry

            lax.fori_loop(0, 2, sum_codes, 0)
        books = [packed_refs[kz][0, 256:257, :] + packed_refs[kz][1, 256:257, :] for kz in range(4)]
        books = jnp.concatenate([books[0] + books[1], books[2] + books[3]], axis=1)
        chosen = jnp.where((iota((512, 256), 0) ^ place) == books, 1.0, 0.0).astype(BF16)
        high, low = split(sums_ref[...].reshape(256, 512))
        total = dot_nn(chosen, high) + dot_nn(chosen, low)
        keep_ref[...] = total[0:256]
        send_ref[...] = total[256:512]


def step(second, place, packed, right, errors, rest):
    def kernel(where_ref, *refs):
        step_body(second, where_ref, refs[0:4], refs[4:6], refs[6:])

    def tile_column(half):
        return lambda n: jnp.clip(2 * n + half, 0, 7)

    right_specs, error_specs = [], []
    height = 104 if second else 64
    for half in (-1, 0):
        right_specs.append(pl.BlockSpec((1, 512, 1024), lambda n, f=tile_column(half): (f(n), 0, 0)))
    for half in (0, 1):
        error_specs += [pl.BlockSpec((2, 1, height, 128), lambda n, f=tile_column(half): (0, f(n), 0, 0))] * 8
    half = jax.ShapeDtypeStruct((256, 512), F32)
    return pl.pallas_call(
        kernel,
        out_shape=[half, half],
        grid=(5,),
        in_specs=[in_smem()]
        + [whole(x) for x in packed]
        + right_specs
        + error_specs
        + [whole(x) for x in rest],
        out_specs=[pl.BlockSpec((256, 512), lambda n: (0, 0))] * 2,
        scratch_shapes=[
            pltpu.VMEM((512, 768), BF16),
            pltpu.VMEM((512, 768), BF16),
            pltpu.VMEM((8, 512, 128), F32),
            pltpu.VMEM((8, 32, 512), F32),
            pltpu.VMEM((512, 512), BF16),
            pltpu.VMEM((512, 512), BF16),
            pltpu.VMEM((2, 32, 128), F32),
            pltpu.VMEM((2, 32, 512), F32),
        ],
        compiler_params=pltpu.CompilerParams(vmem_limit_bytes=VMEM_LIMIT),
        cost_estimate=pl.CostEstimate(flops=STEP_FLOPS, bytes_accessed=16 * 1024 * 1024, transcendentals=0),
    )(place, *packed, right, right, *errors, *errors, *rest)


def update_kernel(where_ref, books_ref, near_ref, far_ref, out_ref):
    for part, ref in enumerate((near_ref, far_ref)):
        for k in range(4):
            start = pl.multiple_of((part * 256 + k * 64) ^ where_ref[2], 64)
            for c in range(2):
                moved = LEARN_RATE * ref[k * 64 : k * 64 + 64, c * 256 : c * 256 + 256]
                out_ref[pl.ds(start, 64), c, :] = books_ref[pl.ds(start, 64), c, :] - moved


def update(where, codebooks, near, far):
    return pl.pallas_call(
        update_kernel,
        out_shape=jax.ShapeDtypeStruct((512, 2, 256), F32),
        in_specs=[in_smem()] + in_vmem(3),
        out_specs=in_vmem(1)[0],
    )(where, codebooks, near, far)


def sum_all(keep, send, *beside):
    half = keep + swap(send, dcore=1)
    quarter = [half[k * 64 : k * 64 + 64] for k in range(4)]
    got = [None] + [swap(quarter[k], dx=k) for k in (1, 2, 3)]
    s = (quarter[0] + got[2]) + (got[1] + got[3])
    s, *beside = hold(s, *beside)
    got = [None] + [swap(s, dyl=k & 1, dyh=k >> 1) for k in (1, 2, 3)]
    s = (s + got[2]) + (got[1] + got[3])
    got = [None] + [swap(s, dz=k) for k in (1, 2, 3)]
    s = (s + got[2]) + (got[1] + got[3])
    near = jnp.concatenate([s] + [swap(s, dx=k) for k in (1, 2, 3)])
    return near, swap(near, dcore=1), *beside


def hold(*values):
    return lax.optimization_barrier(values)


def pair_up(own):
    return jnp.stack([own, swap(own, dyh=1)])


def over_x(pair):
    return [pair] + [swap(pair, dx=k) for k in (1, 2, 3)]


def both_cores(near):
    return list(near) + [swap(v, dcore=1) for v in near]


def per_device(hessian, weights, codes, tile_map, codebooks):
    row, col = lax.axis_index("row").astype(I32), lax.axis_index("col").astype(I32)
    where = jnp.stack([row, col, (col & 1) * 256 + (col >> 2) * 64])
    pieces, own = make_pieces(codes, tile_map)
    pieces = lax.all_to_all(pieces, "col", 0, 0, tiled=True)
    pair = pair_up(first(weights, own, tile_map, codebooks))
    pieces, pair = hold(pieces, pair)

    around = over_x(pair)
    pieces = jnp.stack([pieces, swap(pieces, dyl=1)])
    pieces, later = hold(pieces, where)
    right = split_hessian(later, hessian.reshape(16384, 128))
    packed = sort_codes([pieces], 0)
    right, packed, one, three = hold(right, packed, *[swap(pieces, dz=k) for k in (1, 3)])
    pieces, one = hold(pieces, one)
    two = swap(pieces, dz=2)
    packed_one, packed_three = sort_codes([one], 1), sort_codes([three], 3)
    packed_one, packed_three, *around = hold(packed_one, packed_three, *around)
    around = both_cores(around)
    packed = [*packed, *packed_one, *sort_codes([two], 2), *packed_three]
    keep, send = step(False, where, packed, right, around, [])
    near, far = sum_all(keep, send)
    keep, send = step(True, where, packed, right, around, [near, far])
    near, far, codebooks = sum_all(keep, send, update(where, codebooks, near, far))
    return update(where, codebooks, near, far)


def solution(mesh):
    placed = (P("row", None, "col", None), P("col", "row"), P("col", "row"), P("col", "row"), P())
    return jax.shard_map(per_device, mesh=mesh, in_specs=placed, out_specs=P(), check_vma=False)
```

```python
import jax
import jax.numpy as jnp
from jax import lax
from jax.experimental import pallas as pl
from jax.experimental.pallas import tpu as pltpu
from jax.sharding import PartitionSpec as P

F32 = jnp.float32
BF16 = jnp.bfloat16
I32 = jnp.int32
LEARN_RATE = 0.01
BOTH = ("row", "col")
VMEM_LIMIT = 56 * 1024 * 1024
STEP_FLOPS = 18 * 10**9
SORT_FLOPS = 5 * 10**9
SPLIT_FLOPS = 9 * 10**9


def partners(dx, dyh, dcore, dyl, dz):
    flip_col = dx * 4 + dyh * 2 + dcore
    flip_row = dyl * 4 + dz
    return [(i, i ^ (flip_row * 16 + flip_col)) for i in range(128)]


def swap(v, dx=0, dyh=0, dcore=0, dyl=0, dz=0):
    return lax.ppermute(v, BOTH, partners(dx, dyh, dcore, dyl, dz))


def lanes(x, index):
    return jnp.take_along_axis(x, index, axis=1, mode="promise_in_bounds")


def iota(shape, dim):
    return lax.broadcasted_iota(I32, shape, dim)


def split(x):
    high = x.astype(BF16)
    low = (x - high.astype(F32)).astype(BF16)
    return high, low


def dot_nt(a, b):
    return lax.dot_general(a, b, (((1,), (1,)), ((), ())), preferred_element_type=F32)


def dot_nn(a, b):
    return lax.dot_general(a, b, (((1,), (0,)), ((), ())), preferred_element_type=F32)


def whole(x):
    return pl.BlockSpec(x.shape, lambda *_: (0,) * x.ndim)


def in_vmem(n):
    return [pl.BlockSpec(memory_space=pltpu.VMEM)] * n


def in_smem():
    return pl.BlockSpec(memory_space=pltpu.SMEM)


def lookup(code, low_table, high_table):
    low = code & 127
    return jnp.where(code >= 128, lanes(high_table, low), lanes(low_table, low))


def part_pairs():
    lane = iota((256, 256), 1)
    return jnp.where(iota((256, 256), 0) == 2 * (lane & 127) + (lane >> 7), 1.0, 0.0).astype(BF16)


def tile_rows(start, tile, parity):
    return pl.ds(start + tile * 16 + parity, 8, stride=2)


def pieces_kernel(tile_ref, codes_ref, piece_ref, own_ref, held_ref):
    lane = iota((8, 128), 1)
    left = lane < 64
    for q in range(8):
        cut = slice(q * 128, q * 128 + 128)
        held_ref[q * 32 : q * 32 + 32, :] = codes_ref[:, cut]
        for t in range(2):
            even = held_ref[tile_rows(q * 32, t, 0), :]
            odd = held_ref[tile_rows(q * 32, t, 1), :]
            own_ref[t * 8 : t * 8 + 8, cut] = even
            own_ref[16 + t * 8 : 24 + t * 8, cut] = odd
            pair = [
                jnp.where(left, even, pltpu.roll(odd, 64, 1)),
                jnp.where(left, pltpu.roll(even, 64, 1), odd),
            ]
            for h in range(2):
                piece_ref[2 * q + h, t * 8 : t * 8 + 8, :] = pair[h]
        books = jnp.where((lane & 1) == 0, tile_ref[0, q], tile_ref[1, q])
        for h in range(2):
            piece_ref[2 * q + h, 16:24, :] = books


def make_pieces(codes, tile_map):
    return pl.pallas_call(
        pieces_kernel,
        out_shape=[jax.ShapeDtypeStruct((16, 24, 128), I32), jax.ShapeDtypeStruct((32, 1024), I32)],
        in_specs=[in_smem()] + in_vmem(1),
        out_specs=in_vmem(2),
        scratch_shapes=[pltpu.VMEM((256, 128), I32)],
    )(tile_map, codes)


def first_kernel(tile_ref, weights_ref, own_ref, books_ref, out_ref, weight_ref):
    parting = part_pairs()
    for q in range(8):
        parted = dot_nn(weights_ref[:, q * 256 : q * 256 + 256], parting)
        weight_ref[q * 64 : q * 64 + 32, :] = parted[:, 0:128]
        weight_ref[q * 64 + 32 : q * 64 + 64, :] = parted[:, 128:256]
    for q in range(8):
        for t in range(2):
            book = books_ref[tile_ref[t, q]]
            for c in range(2):
                tables = [jnp.broadcast_to(book[c : c + 1, k * 128 : k * 128 + 128], (8, 128)) for k in range(2)]
                for parity in range(2):
                    row = parity * 16 + t * 8
                    code = own_ref[row : row + 8, q * 128 : q * 128 + 128]
                    weight = weight_ref[tile_rows((q * 2 + c) * 32, t, parity), :]
                    out_ref[q, c * 32 + row : c * 32 + row + 8, :] = lookup(code, *tables) - weight
        out_ref[q, 64:96, :] = own_ref[:, q * 128 : q * 128 + 128].astype(F32)
        out_ref[q, 96:104, :] = jnp.where(iota((8, 128), 0) == 0, tile_ref[0, q], tile_ref[1, q]).astype(F32)


def first(weights, own, tile_map, codebooks):
    return pl.pallas_call(
        first_kernel,
        out_shape=jax.ShapeDtypeStruct((8, 104, 128), F32),
        in_specs=[in_smem()] + in_vmem(3),
        out_specs=in_vmem(1)[0],
        scratch_shapes=[pltpu.VMEM((512, 128), F32)],
    )(tile_map, weights, own, codebooks)


def spot(position):
    return ((position & 15) << 3) | (position >> 4)


def spot_back(lane):
    return ((lane & 7) << 4) | (lane >> 3)


def sort_block(keys):
    rows = [keys[v * 8 : v * 8 + 8, :] for v in range(16)]
    sub = iota((8, 128), 0)
    k = 2
    while k <= 128:
        j = k // 2
        while j >= 1:
            if j < 16:
                for v in range(16):
                    if v & j:
                        continue
                    a, b = rows[v], rows[v | j]
                    small, large = jnp.minimum(a, b), jnp.maximum(a, b)
                    if k < 16:
                        rising = (v & k) == 0
                        rows[v], rows[v | j] = (small, large) if rising else (large, small)
                    elif k == 128:
                        rows[v], rows[v | j] = small, large
                    else:
                        up = (sub & (k >> 4)) == 0
                        rows[v], rows[v | j] = jnp.where(up, small, large), jnp.where(up, large, small)
            else:
                step = j >> 4
                lower = (sub & step) == 0
                up = lower if k == 128 else ((sub & (k >> 4)) == 0) == lower
                for v in range(16):
                    other = jnp.where(lower, pltpu.roll(rows[v], 8 - step, 0), pltpu.roll(rows[v], step, 0))
                    rows[v] = jnp.where(up, jnp.minimum(rows[v], other), jnp.maximum(rows[v], other))
            j //= 2
        k *= 2
    return jnp.concatenate(rows, axis=0)


def sort_codes(pieces, odd_shift):
    many = len(pieces)

    def sort_kernel(*refs):
        packed_ref = refs[many]
        turn = pl.program_id(0)
        piece = refs[0][0]
        for n in range(1, many):
            piece = jnp.where(turn >= 2 * n, refs[n][0], piece)
        lane = iota((256, 128), 1)
        base = odd_shift * 32 + lax.rem(turn, 2) * 16
        books = jnp.zeros((8, 128), I32)
        for origin in range(16):
            books = jnp.where((iota((8, 128), 1) >> 1) == base + origin, piece[origin, 16:24, :], books)
        packed_ref[0, 256:264, :] = books
        key = (piece[:, 0:16, :].reshape(256, 128) * 128 + lane).astype(F32)
        halves = [sort_block(key[h * 128 : h * 128 + 128, :].T).T for h in range(2)]
        code = jnp.concatenate(halves, axis=0).astype(I32)
        counts = []
        for half in range(2):
            limit = (half * 128 + lane + 1) * 128
            count = jnp.zeros((256, 128), I32)
            for step in (64, 32, 16, 8, 4, 2, 1, 1):
                below = lanes(code, spot(count + (step - 1))) < limit
                count = jnp.where(below, count + step, count)
            counts.append(count)
        packed_ref[0, 0:256, :] = (code & 127) | (counts[0] << 8) | (counts[1] << 16)

    return pl.pallas_call(
        sort_kernel,
        out_shape=jax.ShapeDtypeStruct((2 * many, 264, 128), I32),
        grid=(2 * many,),
        in_specs=[pl.BlockSpec((1, 16, 24, 128), lambda j, n=n: (jnp.clip(j - 2 * n, 0, 1), 0, 0, 0)) for n in range(many)],
        out_specs=pl.BlockSpec((1, 264, 128), lambda j: (j, 0, 0)),
        compiler_params=pltpu.CompilerParams(vmem_limit_bytes=VMEM_LIMIT),
        cost_estimate=pl.CostEstimate(flops=many * SORT_FLOPS, bytes_accessed=many * 1024 * 1024, transcendentals=0),
    )(*pieces)


def split_kernel(where_ref, hessian_ref, right_ref):
    for j in range(8):
        for c in range(2):
            high, low = split(hessian_ref[pl.ds(c * 8 + j, 128, stride=16), :])
            cut = slice(j * 128, j * 128 + 128)
            right_ref[0, c * 128 : c * 128 + 128, cut] = high
            right_ref[0, 256 + c * 128 : 256 + c * 128 + 128, cut] = low


def split_hessian(where, rows):
    return pl.pallas_call(
        split_kernel,
        out_shape=jax.ShapeDtypeStruct((8, 512, 1024), BF16),
        grid=(8,),
        in_specs=[in_smem(), pl.BlockSpec((2048, 128), lambda q: (q, 0))],
        out_specs=pl.BlockSpec((1, 512, 1024), lambda q: (q, 0, 0)),
        compiler_params=pltpu.CompilerParams(vmem_limit_bytes=VMEM_LIMIT),
        cost_estimate=pl.CostEstimate(flops=SPLIT_FLOPS, bytes_accessed=20 * 1024 * 1024, transcendentals=0),
    )(where, rows)


def step_body(second, where_ref, packed_refs, rights, refs):
    error_refs, refs = (refs[:8], refs[8:16]), refs[16:]
    if second:
        (near_ref, far_ref), refs = refs[:2], refs[2:]
    keep_ref, send_ref, left0_ref, left1_ref, grad_ref, sums_ref, high_ref, low_ref, ids_ref, table_ref = refs
    n = pl.program_id(0)
    row, col, place = where_ref[0], where_ref[1], where_ref[2]

    def multiply(left_ref, right_ref):
        for part in range(4):
            for m in range(2):
                rows = slice(m * 256, m * 256 + 256)
                cut = slice(part * 256, part * 256 + 256)
                more = dot_nn(left_ref[rows, 0:512], right_ref[0, :, cut]) + dot_nn(left_ref[rows, 512:768], right_ref[0, 0:256, cut])
                grad_ref[2 * part, rows, :] += more[:, 0:128]
                grad_ref[2 * part + 1, rows, :] += more[:, 128:256]

    def prepare(half, left_ref):
        if second:
            for which in range(8):
                for kyh in range(2):
                    at = which * 4 + kyh * 2
                    ids_ref[half, at : at + 2, :] = error_refs[half][which][kyh, 0, 96:98, :]
            ids = ids_ref[half].astype(I32) ^ place
            lane = iota((32, 128), 1)
            chosen = [jnp.where(ids == lane + k * 128, 1.0, 0.0) for k in range(4)]
            chosen = jnp.concatenate(chosen, axis=1).astype(BF16)
            table_ref[half] = LEARN_RATE * (dot_nn(chosen, high_ref[...]) + dot_nn(chosen, low_ref[...]))
        for core in range(2):
            for kx in range(4):
                which = core * 4 + kx
                for kyh in range(2):
                    start = pl.multiple_of((col ^ (kx * 4 + kyh * 2 + core)) * 16, 16)
                    base = which * 4 + kyh * 2
                    for c in range(2):
                        if second:
                            tables = [
                                [
                                    jnp.broadcast_to(table_ref[half, base + t : base + t + 1, (c * 2 + k) * 128 : (c * 2 + k) * 128 + 128], (8, 128))
                                    for k in range(2)
                                ]
                                for t in range(2)
                            ]
                        for parity in range(2):
                            row = c * 32 + parity * 16
                            value = error_refs[half][which][kyh, 0, row : row + 16, :]
                            if second:
                                row = 64 + parity * 16
                                code = error_refs[half][which][kyh, 0, row : row + 16, :].astype(I32)
                                moves = [lookup(code[t * 8 : t * 8 + 8], *tables[t]) for t in range(2)]
                                value = value - jnp.concatenate(moves, axis=0)
                            high, low = split(value)
                            rows = pl.ds(parity * 256 + start, 16)
                            left_ref[rows, c * 128 : c * 128 + 128] = high
                            left_ref[rows, 256 + c * 128 : 256 + c * 128 + 128] = high
                            left_ref[rows, 512 + c * 128 : 512 + c * 128 + 128] = low

    @pl.when(n == 0)
    def _():
        left1_ref[...] = jnp.zeros((512, 768), BF16)
        grad_ref[...] = jnp.zeros((8, 512, 128), F32)
        if second:
            high_ref[0:256, :], low_ref[0:256, :] = split(near_ref[...])
            high_ref[256:512, :], low_ref[256:512, :] = split(far_ref[...])

    prepare(0, left0_ref)
    multiply(left1_ref, rights[0])

    @pl.when(n < 4)
    def _():
        prepare(1, left1_ref)
        multiply(left0_ref, rights[1])

    @pl.when(n == 4)
    def _():
        parting = part_pairs()
        running = jnp.where(spot_back(iota((256, 128), 0) & 127) <= iota((256, 128), 1), 1.0, 0.0).astype(BF16)
        lane = iota((32, 128), 1)
        for kz in range(4):
            for dyl in range(2):
                j = row ^ (dyl * 4 + kz)
                at = kz * 2 + dyl
                both = jnp.concatenate([grad_ref[j, 0:256, :], grad_ref[j, 256:512, :]], axis=1)
                high, low = split(both)
                pairs = dot_nn(high, parting) + dot_nn(low, parting)
                held_ref, first_row = packed_refs[kz]
                packed = held_ref[first_row + dyl, 0:256, :]
                source = packed & 127
                counts = [(packed >> 8) & 255, packed >> 16]
                for c in range(2):
                    ordered = lanes(pairs[:, c * 128 : c * 128 + 128], source)
                    prefix = dot_nn(jnp.concatenate(split(ordered), axis=1), running)
                    upto = []
                    for count in counts:
                        value = jnp.where(count > 0, lanes(prefix, jnp.maximum(count - 1, 0)), 0.0)
                        upto.append(value.reshape(32, 8, 128).sum(axis=1))
                    earlier = [pltpu.roll(v, 1, 1) for v in upto]
                    low_sums = 2.0 * (upto[0] - jnp.where(lane == 0, 0.0, earlier[0]))
                    high_sums = 2.0 * (upto[1] - jnp.where(lane == 0, earlier[0], earlier[1]))
                    sums_ref[at, :, c * 256 : c * 256 + 128] = low_sums
                    sums_ref[at, :, c * 256 + 128 : c * 256 + 256] = high_sums
        books = [ref[first_row, 256:257, :] + ref[first_row + 1, 256:257, :] for ref, first_row in packed_refs]
        books = jnp.concatenate([books[0] + books[1], books[2] + books[3]], axis=1)
        chosen = jnp.where((iota((512, 256), 0) ^ place) == books, 1.0, 0.0).astype(BF16)
        high, low = split(sums_ref[...].reshape(256, 512))
        total = dot_nn(chosen, high) + dot_nn(chosen, low)
        keep_ref[...] = total[0:256]
        send_ref[...] = total[256:512]


def step(second, place, packed, right, errors, rest):
    def kernel(where_ref, *refs):
        zero, odd, two = refs[0:3]
        step_body(second, where_ref, ((zero, 0), (odd, 0), (two, 0), (odd, 2)), refs[3:5], refs[5:])

    def tile_column(half):
        return lambda n: jnp.clip(2 * n + half, 0, 7)

    right_specs, error_specs = [], []
    height = 104 if second else 64
    for half in (-1, 0):
        right_specs.append(pl.BlockSpec((1, 512, 1024), lambda n, f=tile_column(half): (f(n), 0, 0)))
    for half in (0, 1):
        error_specs += [pl.BlockSpec((2, 1, height, 128), lambda n, f=tile_column(half): (0, f(n), 0, 0))] * 8
    half = jax.ShapeDtypeStruct((256, 512), F32)
    return pl.pallas_call(
        kernel,
        out_shape=[half, half],
        grid=(5,),
        in_specs=[in_smem()]
        + [whole(x) for x in packed]
        + right_specs
        + error_specs
        + [whole(x) for x in rest],
        out_specs=[pl.BlockSpec((256, 512), lambda n: (0, 0))] * 2,
        scratch_shapes=[
            pltpu.VMEM((512, 768), BF16),
            pltpu.VMEM((512, 768), BF16),
            pltpu.VMEM((8, 512, 128), F32),
            pltpu.VMEM((8, 32, 512), F32),
            pltpu.VMEM((512, 512), BF16),
            pltpu.VMEM((512, 512), BF16),
            pltpu.VMEM((2, 32, 128), F32),
            pltpu.VMEM((2, 32, 512), F32),
        ],
        compiler_params=pltpu.CompilerParams(vmem_limit_bytes=VMEM_LIMIT),
        cost_estimate=pl.CostEstimate(flops=STEP_FLOPS, bytes_accessed=16 * 1024 * 1024, transcendentals=0),
    )(place, *packed, right, right, *errors, *errors, *rest)


def update_kernel(where_ref, books_ref, near_ref, far_ref, out_ref):
    for part, ref in enumerate((near_ref, far_ref)):

        def block(k, carry, part=part, ref=ref):
            start = pl.multiple_of((part * 256 + k * 64) ^ where_ref[2], 64)
            from_row = pl.multiple_of(k * 64, 64)
            for c in range(2):
                moved = LEARN_RATE * ref[pl.ds(from_row, 64), c * 256 : c * 256 + 256]
                out_ref[pl.ds(start, 64), c, :] = books_ref[pl.ds(start, 64), c, :] - moved
            return carry

        lax.fori_loop(0, 4, block, 0)


def update(where, codebooks, near, far):
    return pl.pallas_call(
        update_kernel,
        out_shape=jax.ShapeDtypeStruct((512, 2, 256), F32),
        in_specs=[in_smem()] + in_vmem(3),
        out_specs=in_vmem(1)[0],
    )(where, codebooks, near, far)


def sum_all(keep, send, *beside):
    half = keep + swap(send, dcore=1)
    quarter = [half[k * 64 : k * 64 + 64] for k in range(4)]
    got = [None] + [swap(quarter[k], dx=k) for k in (1, 2, 3)]
    s = (quarter[0] + got[2]) + (got[1] + got[3])
    s, *beside = hold(s, *beside)
    got = [None] + [swap(s, dyl=k & 1, dyh=k >> 1) for k in (1, 2, 3)]
    s = (s + got[2]) + (got[1] + got[3])
    got = [None] + [swap(s, dz=k) for k in (1, 2, 3)]
    s = (s + got[2]) + (got[1] + got[3])
    near = jnp.concatenate([s] + [swap(s, dx=k) for k in (1, 2, 3)])
    return near, swap(near, dcore=1), *beside


def hold(*values):
    return lax.optimization_barrier(values)


def pair_up(own):
    return jnp.stack([own, swap(own, dyh=1)])


def over_x(pair):
    return [pair] + [swap(pair, dx=k) for k in (1, 2, 3)]


def both_cores(near):
    return list(near) + [swap(v, dcore=1) for v in near]


def per_device(hessian, weights, codes, tile_map, codebooks):
    row, col = lax.axis_index("row").astype(I32), lax.axis_index("col").astype(I32)
    where = jnp.stack([row, col, (col & 1) * 256 + (col >> 2) * 64])
    pieces, own = make_pieces(codes, tile_map)
    pieces = lax.all_to_all(pieces, "col", 0, 0, tiled=True)
    pair = pair_up(first(weights, own, tile_map, codebooks))
    pieces, pair = hold(pieces, pair)

    around = over_x(pair)
    pieces = jnp.stack([pieces, swap(pieces, dyl=1)])
    pieces, later = hold(pieces, where)
    right = split_hessian(later, hessian.reshape(16384, 128))
    packed = sort_codes([pieces], 0)
    right, packed, one, three = hold(right, packed, *[swap(pieces, dz=k) for k in (1, 3)])
    pieces, one = hold(pieces, one)
    two = swap(pieces, dz=2)
    packed_odd, *around = hold(sort_codes([one, three], 1), *around)
    around = both_cores(around)
    packed = [packed, packed_odd, sort_codes([two], 0)]
    keep, send = step(False, where, packed, right, around, [])
    near, far = sum_all(keep, send)
    keep, send = step(True, where, packed, right, around, [near, far])
    near, far, codebooks = sum_all(keep, send, update(where, codebooks, near, far))
    return update(where, codebooks, near, far)


def solution(mesh):
    placed = (P("row", None, "col", None), P("col", "row"), P("col", "row"), P("col", "row"), P())
    return jax.shard_map(per_device, mesh=mesh, in_specs=placed, out_specs=P(), check_vma=False)
```

```python
import jax
import jax.numpy as jnp
from jax import lax
from jax.experimental import pallas as pl
from jax.experimental.pallas import tpu as pltpu
from jax.sharding import PartitionSpec as P

F32 = jnp.float32
BF16 = jnp.bfloat16
I32 = jnp.int32
LEARN_RATE = 0.01
BOTH = ("row", "col")
VMEM_LIMIT = 56 * 1024 * 1024
STEP_FLOPS = 18 * 10**9
SORT_FLOPS = 5 * 10**9
SPLIT_FLOPS = 9 * 10**9


def partners(dx, dyh, dcore, dyl, dz):
    flip_col = dx * 4 + dyh * 2 + dcore
    flip_row = dyl * 4 + dz
    return [(i, i ^ (flip_row * 16 + flip_col)) for i in range(128)]


def swap(v, dx=0, dyh=0, dcore=0, dyl=0, dz=0):
    return lax.ppermute(v, BOTH, partners(dx, dyh, dcore, dyl, dz))


def lanes(x, index):
    return jnp.take_along_axis(x, index, axis=1, mode="promise_in_bounds")


def iota(shape, dim):
    return lax.broadcasted_iota(I32, shape, dim)


def split(x):
    high = x.astype(BF16)
    low = (x - high.astype(F32)).astype(BF16)
    return high, low


def dot_nt(a, b):
    return lax.dot_general(a, b, (((1,), (1,)), ((), ())), preferred_element_type=F32)


def dot_nn(a, b):
    return lax.dot_general(a, b, (((1,), (0,)), ((), ())), preferred_element_type=F32)


def whole(x):
    return pl.BlockSpec(x.shape, lambda *_: (0,) * x.ndim)


def in_vmem(n):
    return [pl.BlockSpec(memory_space=pltpu.VMEM)] * n


def in_smem():
    return pl.BlockSpec(memory_space=pltpu.SMEM)


def lookup(code, low_table, high_table):
    low = code & 127
    return jnp.where(code >= 128, lanes(high_table, low), lanes(low_table, low))


def part_pairs():
    lane = iota((256, 256), 1)
    return jnp.where(iota((256, 256), 0) == 2 * (lane & 127) + (lane >> 7), 1.0, 0.0).astype(BF16)


def tile_rows(start, tile, parity):
    return pl.ds(start + tile * 16 + parity, 8, stride=2)


def make_pieces(tile_ref, codes_ref, piece_ref, own_ref, held_ref):
    lane = iota((8, 128), 1)
    left = lane < 64
    for q in range(8):
        cut = slice(q * 128, q * 128 + 128)
        held_ref[q * 32 : q * 32 + 32, :] = codes_ref[:, cut]
        for t in range(2):
            even = held_ref[tile_rows(q * 32, t, 0), :]
            odd = held_ref[tile_rows(q * 32, t, 1), :]
            own_ref[t * 8 : t * 8 + 8, cut] = even
            own_ref[16 + t * 8 : 24 + t * 8, cut] = odd
            pair = [
                jnp.where(left, even, pltpu.roll(odd, 64, 1)),
                jnp.where(left, pltpu.roll(even, 64, 1), odd),
            ]
            for h in range(2):
                piece_ref[2 * q + h, t * 8 : t * 8 + 8, :] = pair[h]
        books = jnp.where((lane & 1) == 0, tile_ref[0, q], tile_ref[1, q])
        for h in range(2):
            piece_ref[2 * q + h, 16:24, :] = books


def first_kernel(tile_ref, weights_ref, codes_ref, books_ref, out_ref, piece_ref, weight_ref, own_ref, held_ref):
    make_pieces(tile_ref, codes_ref, piece_ref, own_ref, held_ref)
    parting = part_pairs()
    for q in range(8):
        parted = dot_nn(weights_ref[:, q * 256 : q * 256 + 256], parting)
        weight_ref[q * 64 : q * 64 + 32, :] = parted[:, 0:128]
        weight_ref[q * 64 + 32 : q * 64 + 64, :] = parted[:, 128:256]
    for q in range(8):
        for t in range(2):
            book = books_ref[tile_ref[t, q]]
            for c in range(2):
                tables = [jnp.broadcast_to(book[c : c + 1, k * 128 : k * 128 + 128], (8, 128)) for k in range(2)]
                for parity in range(2):
                    row = parity * 16 + t * 8
                    code = own_ref[row : row + 8, q * 128 : q * 128 + 128]
                    weight = weight_ref[tile_rows((q * 2 + c) * 32, t, parity), :]
                    out_ref[q, c * 32 + row : c * 32 + row + 8, :] = lookup(code, *tables) - weight
        out_ref[q, 64:96, :] = own_ref[:, q * 128 : q * 128 + 128].astype(F32)
        out_ref[q, 96:104, :] = jnp.where(iota((8, 128), 0) == 0, tile_ref[0, q], tile_ref[1, q]).astype(F32)


def first(weights, codes, tile_map, codebooks):
    return pl.pallas_call(
        first_kernel,
        out_shape=[jax.ShapeDtypeStruct((8, 104, 128), F32), jax.ShapeDtypeStruct((16, 24, 128), I32)],
        in_specs=[in_smem()] + in_vmem(3),
        out_specs=in_vmem(2),
        scratch_shapes=[pltpu.VMEM((512, 128), F32), pltpu.VMEM((32, 1024), I32), pltpu.VMEM((256, 128), I32)],
    )(tile_map, weights, codes, codebooks)


def spot(position):
    return ((position & 15) << 3) | (position >> 4)


def spot_back(lane):
    return ((lane & 7) << 4) | (lane >> 3)


def sort_block(keys):
    rows = [keys[v * 8 : v * 8 + 8, :] for v in range(16)]
    sub = iota((8, 128), 0)
    k = 2
    while k <= 128:
        j = k // 2
        while j >= 1:
            if j < 16:
                for v in range(16):
                    if v & j:
                        continue
                    a, b = rows[v], rows[v | j]
                    small, large = jnp.minimum(a, b), jnp.maximum(a, b)
                    if k < 16:
                        rising = (v & k) == 0
                        rows[v], rows[v | j] = (small, large) if rising else (large, small)
                    elif k == 128:
                        rows[v], rows[v | j] = small, large
                    else:
                        up = (sub & (k >> 4)) == 0
                        rows[v], rows[v | j] = jnp.where(up, small, large), jnp.where(up, large, small)
            else:
                step = j >> 4
                lower = (sub & step) == 0
                up = lower if k == 128 else ((sub & (k >> 4)) == 0) == lower
                for v in range(16):
                    other = jnp.where(lower, pltpu.roll(rows[v], 8 - step, 0), pltpu.roll(rows[v], step, 0))
                    rows[v] = jnp.where(up, jnp.minimum(rows[v], other), jnp.maximum(rows[v], other))
            j //= 2
        k *= 2
    return jnp.concatenate(rows, axis=0)


def sort_codes(pieces, odd_shift):
    many = len(pieces)

    def sort_kernel(*refs):
        packed_ref = refs[many]
        turn = pl.program_id(0)
        piece = refs[0][0]
        for n in range(1, many):
            piece = jnp.where(turn >= 2 * n, refs[n][0], piece)
        lane = iota((256, 128), 1)
        base = odd_shift * 32 + lax.rem(turn, 2) * 16
        books = jnp.zeros((8, 128), I32)
        for origin in range(16):
            books = jnp.where((iota((8, 128), 1) >> 1) == base + origin, piece[origin, 16:24, :], books)
        packed_ref[0, 256:264, :] = books
        key = (piece[:, 0:16, :].reshape(256, 128) * 128 + lane).astype(F32)
        halves = [sort_block(key[h * 128 : h * 128 + 128, :].T).T for h in range(2)]
        code = jnp.concatenate(halves, axis=0).astype(I32)
        counts = []
        for half in range(2):
            limit = (half * 128 + lane + 1) * 128
            count = jnp.zeros((256, 128), I32)
            for step in (64, 32, 16, 8, 4, 2, 1, 1):
                below = lanes(code, spot(count + (step - 1))) < limit
                count = jnp.where(below, count + step, count)
            counts.append(count)
        packed_ref[0, 0:256, :] = (code & 127) | (counts[0] << 8) | (counts[1] << 16)

    return pl.pallas_call(
        sort_kernel,
        out_shape=jax.ShapeDtypeStruct((2 * many, 264, 128), I32),
        grid=(2 * many,),
        in_specs=[pl.BlockSpec((1, 16, 24, 128), lambda j, n=n: (jnp.clip(j - 2 * n, 0, 1), 0, 0, 0)) for n in range(many)],
        out_specs=pl.BlockSpec((1, 264, 128), lambda j: (j, 0, 0)),
        compiler_params=pltpu.CompilerParams(vmem_limit_bytes=VMEM_LIMIT),
        cost_estimate=pl.CostEstimate(flops=many * SORT_FLOPS, bytes_accessed=many * 1024 * 1024, transcendentals=0),
    )(*pieces)


def split_kernel(where_ref, hessian_ref, right_ref):
    for j in range(8):
        for c in range(2):
            high, low = split(hessian_ref[pl.ds(c * 8 + j, 128, stride=16), :])
            cut = slice(j * 128, j * 128 + 128)
            right_ref[0, c * 128 : c * 128 + 128, cut] = high
            right_ref[0, 256 + c * 128 : 256 + c * 128 + 128, cut] = low


def split_hessian(where, rows):
    return pl.pallas_call(
        split_kernel,
        out_shape=jax.ShapeDtypeStruct((8, 512, 1024), BF16),
        grid=(8,),
        in_specs=[in_smem(), pl.BlockSpec((2048, 128), lambda q: (q, 0))],
        out_specs=pl.BlockSpec((1, 512, 1024), lambda q: (q, 0, 0)),
        compiler_params=pltpu.CompilerParams(vmem_limit_bytes=VMEM_LIMIT),
        cost_estimate=pl.CostEstimate(flops=SPLIT_FLOPS, bytes_accessed=20 * 1024 * 1024, transcendentals=0),
    )(where, rows)


def step_body(second, where_ref, packed_refs, rights, refs):
    error_refs, refs = (refs[:8], refs[8:16]), refs[16:]
    if second:
        (near_ref, far_ref), refs = refs[:2], refs[2:]
    keep_ref, send_ref, left0_ref, left1_ref, grad_ref, sums_ref, high_ref, low_ref, ids_ref, table_ref = refs
    n = pl.program_id(0)
    row, col, place = where_ref[0], where_ref[1], where_ref[2]

    def multiply(left_ref, right_ref):
        for part in range(4):
            for m in range(2):
                rows = slice(m * 256, m * 256 + 256)
                cut = slice(part * 256, part * 256 + 256)
                more = dot_nn(left_ref[rows, 0:512], right_ref[0, :, cut]) + dot_nn(left_ref[rows, 512:768], right_ref[0, 0:256, cut])
                grad_ref[2 * part, rows, :] += more[:, 0:128]
                grad_ref[2 * part + 1, rows, :] += more[:, 128:256]

    def prepare(half, left_ref):
        if second:
            for which in range(8):
                for kyh in range(2):
                    at = which * 4 + kyh * 2
                    ids_ref[half, at : at + 2, :] = error_refs[half][which][kyh, 0, 96:98, :]
            ids = ids_ref[half].astype(I32) ^ place
            lane = iota((32, 128), 1)
            chosen = [jnp.where(ids == lane + k * 128, 1.0, 0.0) for k in range(4)]
            chosen = jnp.concatenate(chosen, axis=1).astype(BF16)
            table_ref[half] = LEARN_RATE * (dot_nn(chosen, high_ref[...]) + dot_nn(chosen, low_ref[...]))
        for core in range(2):
            for kx in range(4):
                which = core * 4 + kx
                for kyh in range(2):
                    start = pl.multiple_of((col ^ (kx * 4 + kyh * 2 + core)) * 16, 16)
                    base = which * 4 + kyh * 2
                    for c in range(2):
                        if second:
                            tables = [
                                [
                                    jnp.broadcast_to(table_ref[half, base + t : base + t + 1, (c * 2 + k) * 128 : (c * 2 + k) * 128 + 128], (8, 128))
                                    for k in range(2)
                                ]
                                for t in range(2)
                            ]
                        for parity in range(2):
                            row = c * 32 + parity * 16
                            value = error_refs[half][which][kyh, 0, row : row + 16, :]
                            if second:
                                row = 64 + parity * 16
                                code = error_refs[half][which][kyh, 0, row : row + 16, :].astype(I32)
                                moves = [lookup(code[t * 8 : t * 8 + 8], *tables[t]) for t in range(2)]
                                value = value - jnp.concatenate(moves, axis=0)
                            high, low = split(value)
                            rows = pl.ds(parity * 256 + start, 16)
                            left_ref[rows, c * 128 : c * 128 + 128] = high
                            left_ref[rows, 256 + c * 128 : 256 + c * 128 + 128] = high
                            left_ref[rows, 512 + c * 128 : 512 + c * 128 + 128] = low

    @pl.when(n == 0)
    def _():
        left1_ref[...] = jnp.zeros((512, 768), BF16)
        grad_ref[...] = jnp.zeros((8, 512, 128), F32)
        if second:
            high_ref[0:256, :], low_ref[0:256, :] = split(near_ref[...])
            high_ref[256:512, :], low_ref[256:512, :] = split(far_ref[...])

    prepare(0, left0_ref)
    multiply(left1_ref, rights[0])

    @pl.when(n < 4)
    def _():
        prepare(1, left1_ref)
        multiply(left0_ref, rights[1])

    @pl.when(n == 4)
    def _():
        parting = part_pairs()
        running = jnp.where(spot_back(iota((256, 128), 0) & 127) <= iota((256, 128), 1), 1.0, 0.0).astype(BF16)
        lane = iota((32, 128), 1)
        for kz in range(4):
            for dyl in range(2):
                j = row ^ (dyl * 4 + kz)
                at = kz * 2 + dyl
                both = jnp.concatenate([grad_ref[j, 0:256, :], grad_ref[j, 256:512, :]], axis=1)
                high, low = split(both)
                pairs = dot_nn(high, parting) + dot_nn(low, parting)
                held_ref, first_row = packed_refs[kz]
                packed = held_ref[first_row + dyl, 0:256, :]
                source = packed & 127
                counts = [(packed >> 8) & 255, packed >> 16]
                for c in range(2):
                    ordered = lanes(pairs[:, c * 128 : c * 128 + 128], source)
                    prefix = dot_nn(jnp.concatenate(split(ordered), axis=1), running)
                    upto = []
                    for count in counts:
                        value = jnp.where(count > 0, lanes(prefix, jnp.maximum(count - 1, 0)), 0.0)
                        upto.append(value.reshape(32, 8, 128).sum(axis=1))
                    earlier = [pltpu.roll(v, 1, 1) for v in upto]
                    low_sums = 2.0 * (upto[0] - jnp.where(lane == 0, 0.0, earlier[0]))
                    high_sums = 2.0 * (upto[1] - jnp.where(lane == 0, earlier[0], earlier[1]))
                    sums_ref[at, :, c * 256 : c * 256 + 128] = low_sums
                    sums_ref[at, :, c * 256 + 128 : c * 256 + 256] = high_sums
        books = [ref[first_row, 256:257, :] + ref[first_row + 1, 256:257, :] for ref, first_row in packed_refs]
        books = jnp.concatenate([books[0] + books[1], books[2] + books[3]], axis=1)
        chosen = jnp.where((iota((512, 256), 0) ^ place) == books, 1.0, 0.0).astype(BF16)
        high, low = split(sums_ref[...].reshape(256, 512))
        total = dot_nn(chosen, high) + dot_nn(chosen, low)
        keep_ref[...] = total[0:256]
        send_ref[...] = total[256:512]


def step(second, place, packed, right, errors, rest):
    def kernel(where_ref, *refs):
        zero, odd, two = refs[0:3]
        step_body(second, where_ref, ((zero, 0), (odd, 0), (two, 0), (odd, 2)), refs[3:5], refs[5:])

    def tile_column(half):
        return lambda n: jnp.clip(2 * n + half, 0, 7)

    right_specs, error_specs = [], []
    height = 104 if second else 64
    for half in (-1, 0):
        right_specs.append(pl.BlockSpec((1, 512, 1024), lambda n, f=tile_column(half): (f(n), 0, 0)))
    for half in (0, 1):
        error_specs += [pl.BlockSpec((2, 1, height, 128), lambda n, f=tile_column(half): (0, f(n), 0, 0))] * 8
    half = jax.ShapeDtypeStruct((256, 512), F32)
    return pl.pallas_call(
        kernel,
        out_shape=[half, half],
        grid=(5,),
        in_specs=[in_smem()]
        + [whole(x) for x in packed]
        + right_specs
        + error_specs
        + [whole(x) for x in rest],
        out_specs=[pl.BlockSpec((256, 512), lambda n: (0, 0))] * 2,
        scratch_shapes=[
            pltpu.VMEM((512, 768), BF16),
            pltpu.VMEM((512, 768), BF16),
            pltpu.VMEM((8, 512, 128), F32),
            pltpu.VMEM((8, 32, 512), F32),
            pltpu.VMEM((512, 512), BF16),
            pltpu.VMEM((512, 512), BF16),
            pltpu.VMEM((2, 32, 128), F32),
            pltpu.VMEM((2, 32, 512), F32),
        ],
        compiler_params=pltpu.CompilerParams(vmem_limit_bytes=VMEM_LIMIT),
        cost_estimate=pl.CostEstimate(flops=STEP_FLOPS, bytes_accessed=16 * 1024 * 1024, transcendentals=0),
    )(place, *packed, right, right, *errors, *errors, *rest)


def update_kernel(where_ref, books_ref, near_ref, far_ref, out_ref):
    for part, ref in enumerate((near_ref, far_ref)):

        def block(k, carry, part=part, ref=ref):
            start = pl.multiple_of((part * 256 + k * 64) ^ where_ref[2], 64)
            from_row = pl.multiple_of(k * 64, 64)
            for c in range(2):
                moved = LEARN_RATE * ref[pl.ds(from_row, 64), c * 256 : c * 256 + 256]
                out_ref[pl.ds(start, 64), c, :] = books_ref[pl.ds(start, 64), c, :] - moved
            return carry

        lax.fori_loop(0, 4, block, 0)


def update(where, codebooks, near, far):
    return pl.pallas_call(
        update_kernel,
        out_shape=jax.ShapeDtypeStruct((512, 2, 256), F32),
        in_specs=[in_smem()] + in_vmem(3),
        out_specs=in_vmem(1)[0],
    )(where, codebooks, near, far)


def sum_all(keep, send, *beside):
    half = keep + swap(send, dcore=1)
    quarter = [half[k * 64 : k * 64 + 64] for k in range(4)]
    got = [None] + [swap(quarter[k], dx=k) for k in (1, 2, 3)]
    s = (quarter[0] + got[2]) + (got[1] + got[3])
    s, *beside = hold(s, *beside)
    got = [None] + [swap(s, dyl=k & 1, dyh=k >> 1) for k in (1, 2, 3)]
    s = (s + got[2]) + (got[1] + got[3])
    got = [None] + [swap(s, dz=k) for k in (1, 2, 3)]
    s = (s + got[2]) + (got[1] + got[3])
    near = jnp.concatenate([s] + [swap(s, dx=k) for k in (1, 2, 3)])
    return near, swap(near, dcore=1), *beside


def hold(*values):
    return lax.optimization_barrier(values)


def pair_up(own):
    return jnp.stack([own, swap(own, dyh=1)])


def over_x(pair):
    return [pair] + [swap(pair, dx=k) for k in (1, 2, 3)]


def both_cores(near):
    return list(near) + [swap(v, dcore=1) for v in near]


def per_device(hessian, weights, codes, tile_map, codebooks):
    row, col = lax.axis_index("row").astype(I32), lax.axis_index("col").astype(I32)
    where = jnp.stack([row, col, (col & 1) * 256 + (col >> 2) * 64])
    mine, pieces = first(weights, codes, tile_map, codebooks)
    pieces = lax.all_to_all(pieces, "col", 0, 0, tiled=True)
    pair = pair_up(mine)
    pieces, pair = hold(pieces, pair)

    around = over_x(pair)
    pieces = jnp.stack([pieces, swap(pieces, dyl=1)])
    pieces, later = hold(pieces, where)
    right = split_hessian(later, hessian.reshape(16384, 128))
    packed = sort_codes([pieces], 0)
    right, packed, one, three = hold(right, packed, *[swap(pieces, dz=k) for k in (1, 3)])
    pieces, one = hold(pieces, one)
    two = swap(pieces, dz=2)
    packed_odd, *around = hold(sort_codes([one, three], 1), *around)
    around = both_cores(around)
    packed = [packed, packed_odd, sort_codes([two], 0)]
    keep, send = step(False, where, packed, right, around, [])
    near, far = sum_all(keep, send)
    keep, send = step(True, where, packed, right, around, [near, far])
    near, far, codebooks = sum_all(keep, send, update(where, codebooks, near, far))
    return update(where, codebooks, near, far)


def solution(mesh):
    placed = (P("row", None, "col", None), P("col", "row"), P("col", "row"), P("col", "row"), P())
    return jax.shard_map(per_device, mesh=mesh, in_specs=placed, out_specs=P(), check_vma=False)
```

```python
import jax
import jax.numpy as jnp
from jax import lax
from jax.experimental import pallas as pl
from jax.experimental.pallas import tpu as pltpu
from jax.sharding import PartitionSpec as P

F32 = jnp.float32
BF16 = jnp.bfloat16
I32 = jnp.int32
LEARN_RATE = 0.01
BOTH = ("row", "col")
VMEM_LIMIT = 56 * 1024 * 1024
STEP_FLOPS = 18 * 10**9
SORT_FLOPS = 5 * 10**9
SPLIT_FLOPS = 9 * 10**9


def partners(dx, dyh, dcore, dyl, dz):
    flip_col = dx * 4 + dyh * 2 + dcore
    flip_row = dyl * 4 + dz
    return [(i, i ^ (flip_row * 16 + flip_col)) for i in range(128)]


def swap(v, dx=0, dyh=0, dcore=0, dyl=0, dz=0):
    return lax.ppermute(v, BOTH, partners(dx, dyh, dcore, dyl, dz))


def lanes(x, index):
    return jnp.take_along_axis(x, index, axis=1, mode="promise_in_bounds")


def iota(shape, dim):
    return lax.broadcasted_iota(I32, shape, dim)


def split(x):
    high = x.astype(BF16)
    low = (x - high.astype(F32)).astype(BF16)
    return high, low


def dot_nt(a, b):
    return lax.dot_general(a, b, (((1,), (1,)), ((), ())), preferred_element_type=F32)


def dot_nn(a, b):
    return lax.dot_general(a, b, (((1,), (0,)), ((), ())), preferred_element_type=F32)


def whole(x):
    return pl.BlockSpec(x.shape, lambda *_: (0,) * x.ndim)


def in_vmem(n):
    return [pl.BlockSpec(memory_space=pltpu.VMEM)] * n


def in_smem():
    return pl.BlockSpec(memory_space=pltpu.SMEM)


def lookup(code, low_table, high_table):
    low = code & 127
    return jnp.where(code >= 128, lanes(high_table, low), lanes(low_table, low))


def part_pairs():
    lane = iota((256, 256), 1)
    return jnp.where(iota((256, 256), 0) == 2 * (lane & 127) + (lane >> 7), 1.0, 0.0).astype(BF16)


def tile_rows(start, tile, parity):
    return pl.ds(start + tile * 16 + parity, 8, stride=2)


def make_pieces(tile_ref, codes_ref, piece_ref, own_ref, held_ref):
    lane = iota((8, 128), 1)
    left = lane < 64
    for q in range(8):
        cut = slice(q * 128, q * 128 + 128)
        held_ref[q * 32 : q * 32 + 32, :] = codes_ref[:, cut]
        for t in range(2):
            even = held_ref[tile_rows(q * 32, t, 0), :]
            odd = held_ref[tile_rows(q * 32, t, 1), :]
            own_ref[t * 8 : t * 8 + 8, cut] = even
            own_ref[16 + t * 8 : 24 + t * 8, cut] = odd
            pair = [
                jnp.where(left, even, pltpu.roll(odd, 64, 1)),
                jnp.where(left, pltpu.roll(even, 64, 1), odd),
            ]
            for h in range(2):
                piece_ref[2 * q + h, t * 8 : t * 8 + 8, :] = pair[h]
        books = jnp.where((lane & 1) == 0, tile_ref[0, q], tile_ref[1, q])
        for h in range(2):
            piece_ref[2 * q + h, 16:24, :] = books


def first_kernel(tile_ref, weights_ref, codes_ref, books_ref, out_ref, piece_ref, weight_ref, own_ref, held_ref):
    make_pieces(tile_ref, codes_ref, piece_ref, own_ref, held_ref)
    parting = part_pairs()
    for q in range(8):
        parted = dot_nn(weights_ref[:, q * 256 : q * 256 + 256], parting)
        weight_ref[q * 64 : q * 64 + 32, :] = parted[:, 0:128]
        weight_ref[q * 64 + 32 : q * 64 + 64, :] = parted[:, 128:256]
    for q in range(8):
        for t in range(2):
            book = books_ref[tile_ref[t, q]]
            for c in range(2):
                tables = [jnp.broadcast_to(book[c : c + 1, k * 128 : k * 128 + 128], (8, 128)) for k in range(2)]
                for parity in range(2):
                    row = parity * 16 + t * 8
                    code = own_ref[row : row + 8, q * 128 : q * 128 + 128]
                    weight = weight_ref[tile_rows((q * 2 + c) * 32, t, parity), :]
                    out_ref[q, c * 32 + row : c * 32 + row + 8, :] = lookup(code, *tables) - weight
        out_ref[q, 64:96, :] = own_ref[:, q * 128 : q * 128 + 128].astype(F32)
        out_ref[q, 96:104, :] = jnp.where(iota((8, 128), 0) == 0, tile_ref[0, q], tile_ref[1, q]).astype(F32)


def first(weights, codes, tile_map, codebooks):
    return pl.pallas_call(
        first_kernel,
        out_shape=[jax.ShapeDtypeStruct((8, 104, 128), F32), jax.ShapeDtypeStruct((16, 24, 128), I32)],
        in_specs=[in_smem()] + in_vmem(3),
        out_specs=in_vmem(2),
        scratch_shapes=[pltpu.VMEM((512, 128), F32), pltpu.VMEM((32, 1024), I32), pltpu.VMEM((256, 128), I32)],
    )(tile_map, weights, codes, codebooks)


def spot(position):
    return ((position & 15) << 3) | (position >> 4)


def spot_back(lane):
    return ((lane & 7) << 4) | (lane >> 3)


def sort_block(keys):
    rows = [keys[v * 8 : v * 8 + 8, :] for v in range(16)]
    sub = iota((8, 128), 0)
    k = 2
    while k <= 128:
        j = k // 2
        while j >= 1:
            if j < 16:
                for v in range(16):
                    if v & j:
                        continue
                    a, b = rows[v], rows[v | j]
                    small, large = jnp.minimum(a, b), jnp.maximum(a, b)
                    if k < 16:
                        rising = (v & k) == 0
                        rows[v], rows[v | j] = (small, large) if rising else (large, small)
                    elif k == 128:
                        rows[v], rows[v | j] = small, large
                    else:
                        up = (sub & (k >> 4)) == 0
                        rows[v], rows[v | j] = jnp.where(up, small, large), jnp.where(up, large, small)
            else:
                step = j >> 4
                lower = (sub & step) == 0
                up = lower if k == 128 else ((sub & (k >> 4)) == 0) == lower
                for v in range(16):
                    other = jnp.where(lower, pltpu.roll(rows[v], 8 - step, 0), pltpu.roll(rows[v], step, 0))
                    rows[v] = jnp.where(up, jnp.minimum(rows[v], other), jnp.maximum(rows[v], other))
            j //= 2
        k *= 2
    return jnp.concatenate(rows, axis=0)


def sort_codes(pieces, odd_shift):
    many = len(pieces)

    def sort_kernel(*refs):
        packed_ref = refs[many]
        turn = pl.program_id(0)
        piece = refs[0][0]
        for n in range(1, many):
            piece = jnp.where(turn >= 2 * n, refs[n][0], piece)
        lane = iota((256, 128), 1)
        base = odd_shift * 32 + lax.rem(turn, 2) * 16
        books = jnp.zeros((8, 128), I32)
        for origin in range(16):
            books = jnp.where((iota((8, 128), 1) >> 1) == base + origin, piece[origin, 16:24, :], books)
        packed_ref[0, 256:264, :] = books
        key = (piece[:, 0:16, :].reshape(256, 128) * 128 + lane).astype(F32)
        halves = [sort_block(key[h * 128 : h * 128 + 128, :].T).T for h in range(2)]
        code = jnp.concatenate(halves, axis=0).astype(I32)
        counts = []
        for half in range(2):
            limit = (half * 128 + lane + 1) * 128
            count = jnp.where(code[:, spot(63) : spot(63) + 1] < limit, 64, 0)
            for step in (32, 16, 8, 4, 2, 1, 1):
                below = lanes(code, spot(count + (step - 1))) < limit
                count = jnp.where(below, count + step, count)
            counts.append(count)
        packed_ref[0, 0:256, :] = (code & 127) | (counts[0] << 8) | (counts[1] << 16)

    return pl.pallas_call(
        sort_kernel,
        out_shape=jax.ShapeDtypeStruct((2 * many, 264, 128), I32),
        grid=(2 * many,),
        in_specs=[pl.BlockSpec((1, 16, 24, 128), lambda j, n=n: (jnp.clip(j - 2 * n, 0, 1), 0, 0, 0)) for n in range(many)],
        out_specs=pl.BlockSpec((1, 264, 128), lambda j: (j, 0, 0)),
        compiler_params=pltpu.CompilerParams(vmem_limit_bytes=VMEM_LIMIT),
        cost_estimate=pl.CostEstimate(flops=many * SORT_FLOPS, bytes_accessed=many * 1024 * 1024, transcendentals=0),
    )(*pieces)


def split_kernel(where_ref, hessian_ref, right_ref):
    for j in range(8):
        for c in range(2):
            high, low = split(hessian_ref[pl.ds(c * 8 + j, 128, stride=16), :])
            cut = slice(j * 128, j * 128 + 128)
            right_ref[0, c * 128 : c * 128 + 128, cut] = high
            right_ref[0, 256 + c * 128 : 256 + c * 128 + 128, cut] = low


def split_hessian(where, rows):
    return pl.pallas_call(
        split_kernel,
        out_shape=jax.ShapeDtypeStruct((8, 512, 1024), BF16),
        grid=(8,),
        in_specs=[in_smem(), pl.BlockSpec((2048, 128), lambda q: (q, 0))],
        out_specs=pl.BlockSpec((1, 512, 1024), lambda q: (q, 0, 0)),
        compiler_params=pltpu.CompilerParams(vmem_limit_bytes=VMEM_LIMIT),
        cost_estimate=pl.CostEstimate(flops=SPLIT_FLOPS, bytes_accessed=20 * 1024 * 1024, transcendentals=0),
    )(where, rows)


def step_body(second, where_ref, packed_refs, rights, refs):
    error_refs, refs = (refs[:8], refs[8:16]), refs[16:]
    if second:
        (near_ref, far_ref), refs = refs[:2], refs[2:]
    keep_ref, send_ref, left0_ref, left1_ref, grad_ref, sums_ref, high_ref, low_ref, ids_ref, table_ref = refs
    n = pl.program_id(0)
    row, col, place = where_ref[0], where_ref[1], where_ref[2]

    def multiply(left_ref, right_ref):
        for part in range(4):
            for m in range(2):
                rows = slice(m * 256, m * 256 + 256)
                cut = slice(part * 256, part * 256 + 256)
                more = dot_nn(left_ref[rows, 0:512], right_ref[0, :, cut]) + dot_nn(left_ref[rows, 512:768], right_ref[0, 0:256, cut])
                grad_ref[2 * part, rows, :] += more[:, 0:128]
                grad_ref[2 * part + 1, rows, :] += more[:, 128:256]

    def prepare(half, left_ref):
        if second:
            for which in range(8):
                for kyh in range(2):
                    at = which * 4 + kyh * 2
                    ids_ref[half, at : at + 2, :] = error_refs[half][which][kyh, 0, 96:98, :]
            ids = ids_ref[half].astype(I32) ^ place
            lane = iota((32, 128), 1)
            chosen = [jnp.where(ids == lane + k * 128, 1.0, 0.0) for k in range(4)]
            chosen = jnp.concatenate(chosen, axis=1).astype(BF16)
            table_ref[half] = LEARN_RATE * (dot_nn(chosen, high_ref[...]) + dot_nn(chosen, low_ref[...]))
        for core in range(2):
            for kx in range(4):
                which = core * 4 + kx
                for kyh in range(2):
                    start = pl.multiple_of((col ^ (kx * 4 + kyh * 2 + core)) * 16, 16)
                    base = which * 4 + kyh * 2
                    for c in range(2):
                        if second:
                            tables = [
                                [
                                    jnp.broadcast_to(table_ref[half, base + t : base + t + 1, (c * 2 + k) * 128 : (c * 2 + k) * 128 + 128], (8, 128))
                                    for k in range(2)
                                ]
                                for t in range(2)
                            ]
                        for parity in range(2):
                            row = c * 32 + parity * 16
                            value = error_refs[half][which][kyh, 0, row : row + 16, :]
                            if second:
                                row = 64 + parity * 16
                                code = error_refs[half][which][kyh, 0, row : row + 16, :].astype(I32)
                                moves = [lookup(code[t * 8 : t * 8 + 8], *tables[t]) for t in range(2)]
                                value = value - jnp.concatenate(moves, axis=0)
                            high, low = split(value)
                            rows = pl.ds(parity * 256 + start, 16)
                            left_ref[rows, c * 128 : c * 128 + 128] = high
                            left_ref[rows, 256 + c * 128 : 256 + c * 128 + 128] = high
                            left_ref[rows, 512 + c * 128 : 512 + c * 128 + 128] = low

    @pl.when(n == 0)
    def _():
        left1_ref[...] = jnp.zeros((512, 768), BF16)
        grad_ref[...] = jnp.zeros((8, 512, 128), F32)
        if second:
            high_ref[0:256, :], low_ref[0:256, :] = split(near_ref[...])
            high_ref[256:512, :], low_ref[256:512, :] = split(far_ref[...])

    prepare(0, left0_ref)
    multiply(left1_ref, rights[0])

    @pl.when(n < 4)
    def _():
        prepare(1, left1_ref)
        multiply(left0_ref, rights[1])

    @pl.when(n == 4)
    def _():
        parting = part_pairs()
        running = jnp.where(spot_back(iota((256, 128), 0) & 127) <= iota((256, 128), 1), 1.0, 0.0).astype(BF16)
        lane = iota((32, 128), 1)
        for kz in range(4):
            for dyl in range(2):
                j = row ^ (dyl * 4 + kz)
                at = kz * 2 + dyl
                both = jnp.concatenate([grad_ref[j, 0:256, :], grad_ref[j, 256:512, :]], axis=1)
                high, low = split(both)
                pairs = dot_nn(high, parting) + dot_nn(low, parting)
                held_ref, first_row = packed_refs[kz]
                packed = held_ref[first_row + dyl, 0:256, :]
                source = packed & 127
                counts = [(packed >> 8) & 255, packed >> 16]
                for c in range(2):
                    ordered = lanes(pairs[:, c * 128 : c * 128 + 128], source)
                    prefix = dot_nn(jnp.concatenate(split(ordered), axis=1), running)
                    upto = []
                    for count in counts:
                        value = jnp.where(count > 0, lanes(prefix, jnp.maximum(count - 1, 0)), 0.0)
                        upto.append(value.reshape(32, 8, 128).sum(axis=1))
                    earlier = [pltpu.roll(v, 1, 1) for v in upto]
                    low_sums = 2.0 * (upto[0] - jnp.where(lane == 0, 0.0, earlier[0]))
                    high_sums = 2.0 * (upto[1] - jnp.where(lane == 0, earlier[0], earlier[1]))
                    sums_ref[at, :, c * 256 : c * 256 + 128] = low_sums
                    sums_ref[at, :, c * 256 + 128 : c * 256 + 256] = high_sums
        books = [ref[first_row, 256:257, :] + ref[first_row + 1, 256:257, :] for ref, first_row in packed_refs]
        books = jnp.concatenate([books[0] + books[1], books[2] + books[3]], axis=1)
        chosen = jnp.where((iota((512, 256), 0) ^ place) == books, 1.0, 0.0).astype(BF16)
        high, low = split(sums_ref[...].reshape(256, 512))
        total = dot_nn(chosen, high) + dot_nn(chosen, low)
        keep_ref[...] = total[0:256]
        send_ref[...] = total[256:512]


def step(second, place, packed, right, errors, rest):
    def kernel(where_ref, *refs):
        zero, odd, two = refs[0:3]
        step_body(second, where_ref, ((zero, 0), (odd, 0), (two, 0), (odd, 2)), refs[3:5], refs[5:])

    def tile_column(half):
        return lambda n: jnp.clip(2 * n + half, 0, 7)

    right_specs, error_specs = [], []
    height = 104 if second else 64
    for half in (-1, 0):
        right_specs.append(pl.BlockSpec((1, 512, 1024), lambda n, f=tile_column(half): (f(n), 0, 0)))
    for half in (0, 1):
        error_specs += [pl.BlockSpec((2, 1, height, 128), lambda n, f=tile_column(half): (0, f(n), 0, 0))] * 8
    half = jax.ShapeDtypeStruct((256, 512), F32)
    return pl.pallas_call(
        kernel,
        out_shape=[half, half],
        grid=(5,),
        in_specs=[in_smem()]
        + [whole(x) for x in packed]
        + right_specs
        + error_specs
        + [whole(x) for x in rest],
        out_specs=[pl.BlockSpec((256, 512), lambda n: (0, 0))] * 2,
        scratch_shapes=[
            pltpu.VMEM((512, 768), BF16),
            pltpu.VMEM((512, 768), BF16),
            pltpu.VMEM((8, 512, 128), F32),
            pltpu.VMEM((8, 32, 512), F32),
            pltpu.VMEM((512, 512), BF16),
            pltpu.VMEM((512, 512), BF16),
            pltpu.VMEM((2, 32, 128), F32),
            pltpu.VMEM((2, 32, 512), F32),
        ],
        compiler_params=pltpu.CompilerParams(vmem_limit_bytes=VMEM_LIMIT),
        cost_estimate=pl.CostEstimate(flops=STEP_FLOPS, bytes_accessed=16 * 1024 * 1024, transcendentals=0),
    )(place, *packed, right, right, *errors, *errors, *rest)


def update_kernel(where_ref, books_ref, near_ref, far_ref, out_ref):
    for part, ref in enumerate((near_ref, far_ref)):

        def block(k, carry, part=part, ref=ref):
            start = pl.multiple_of((part * 256 + k * 64) ^ where_ref[2], 64)
            from_row = pl.multiple_of(k * 64, 64)
            for c in range(2):
                moved = LEARN_RATE * ref[pl.ds(from_row, 64), c * 256 : c * 256 + 256]
                out_ref[pl.ds(start, 64), c, :] = books_ref[pl.ds(start, 64), c, :] - moved
            return carry

        lax.fori_loop(0, 4, block, 0)


def update(where, codebooks, near, far):
    return pl.pallas_call(
        update_kernel,
        out_shape=jax.ShapeDtypeStruct((512, 2, 256), F32),
        in_specs=[in_smem()] + in_vmem(3),
        out_specs=in_vmem(1)[0],
    )(where, codebooks, near, far)


def sum_all(keep, send, *beside):
    half = keep + swap(send, dcore=1)
    quarter = [half[k * 64 : k * 64 + 64] for k in range(4)]
    got = [None] + [swap(quarter[k], dx=k) for k in (1, 2, 3)]
    s = (quarter[0] + got[2]) + (got[1] + got[3])
    s, *beside = hold(s, *beside)
    got = [None] + [swap(s, dyl=k & 1, dyh=k >> 1) for k in (1, 2, 3)]
    s = (s + got[2]) + (got[1] + got[3])
    got = [None] + [swap(s, dz=k) for k in (1, 2, 3)]
    s = (s + got[2]) + (got[1] + got[3])
    near = jnp.concatenate([s] + [swap(s, dx=k) for k in (1, 2, 3)])
    return near, swap(near, dcore=1), *beside


def hold(*values):
    return lax.optimization_barrier(values)


def pair_up(own):
    return jnp.stack([own, swap(own, dyh=1)])


def over_x(pair):
    return [pair] + [swap(pair, dx=k) for k in (1, 2, 3)]


def both_cores(near):
    return list(near) + [swap(v, dcore=1) for v in near]


def per_device(hessian, weights, codes, tile_map, codebooks):
    row, col = lax.axis_index("row").astype(I32), lax.axis_index("col").astype(I32)
    where = jnp.stack([row, col, (col & 1) * 256 + (col >> 2) * 64])
    mine, pieces = first(weights, codes, tile_map, codebooks)
    pieces = lax.all_to_all(pieces, "col", 0, 0, tiled=True)
    pair = pair_up(mine)
    pieces, pair, where = hold(pieces, pair, where)

    around = over_x(pair)
    pieces = jnp.stack([pieces, swap(pieces, dyl=1)])
    pieces, later = hold(pieces, where)
    right = split_hessian(later, hessian.reshape(16384, 128))
    packed = sort_codes([pieces], 0)
    right, packed, one, three = hold(right, packed, *[swap(pieces, dz=k) for k in (1, 3)])
    pieces, one = hold(pieces, one)
    two = swap(pieces, dz=2)
    packed_odd, *around = hold(sort_codes([one, three], 1), *around)
    around = both_cores(around)
    packed = [packed, packed_odd, sort_codes([two], 0)]
    keep, send = step(False, where, packed, right, around, [])
    near, far = sum_all(keep, send)
    keep, send = step(True, where, packed, right, around, [near, far])
    near, far, codebooks = sum_all(keep, send, update(where, codebooks, near, far))
    return update(where, codebooks, near, far)


def solution(mesh):
    placed = (P("row", None, "col", None), P("col", "row"), P("col", "row"), P("col", "row"), P())
    return jax.shard_map(per_device, mesh=mesh, in_specs=placed, out_specs=P(), check_vma=False)
```
